32 devices in a mesh: gx: 4 (over y, core), gy: 8 (over z, x).
Axes of the slice: x: 2, y: 2, z: 4, core: 2. Of those that a mesh axis runs over, the one named last changes fastest.
Arguments:
- model_state: float32 [3, 8, 1536, 1024], P(None, None, 'gx', 'gy'), may hold values from -6 to 6
- obs_val: float32 [4096, 384], P(('gx', 'gy')), may hold values from -6 to 6
- obs_owner: int32 [4096, 1], P(('gx', 'gy')), may hold values from 0 to 7; in each aligned block of 128 rows (0 to 127, 128 to 255, ...) at most 32 rows name the same one
- obs_x: int32 [4096], P(('gx', 'gy')), may hold values from 0 to 1535
- obs_y: int32 [4096], P(('gx', 'gy')), may hold values from 0 to 127
- cressman: float32 [1536, 1536], P(None, 'gx'), as said below
- vertical: float32 [3, 8, 128], replicated, may hold values from -2 to 2
Outputs:
- new_state: float32 [3, 8, 1536, 1024], P(None, None, 'gx', 'gy')
The draws below stay inside these ranges and needn't reach their ends.
Inputs may be any that keep to these rules, and one draw needn't show every extreme that they name: `obs_owner`: among the rows of one device, at most 32 name one column; in every draw some device's rows name some column exactly 32 times. `cressman`: entries are positive.
All inputs are finite; a program needn't handle non-finite values.
Results may differ from the reference program's by a relative error of at most 0.0001.
Values sent between devices are 32-bit elements; how exact they have to be, the bound alone decides.
No kernel may reach another device: no remote copies, remote signals or barrier semaphores. Data moves between devices by JAX's collectives and lax.ppermute only.
A program may use at most 128 MiB of HBM per device.

```python
import math
import jax
import jax.numpy as jnp
import numpy as np
from jax import lax

CX = 384
CY = 128
NZ = 8
OBS_LEV = 128
REC_DEV = 128
CAPY = 32
NX = 1536
NY = 1024
RECS = 4096
N_GY = 8


def draw_cressman(key, part):
    rows = jnp.arange(NX, dtype=jnp.float32)[:, None]
    cols = jnp.arange(NX, dtype=jnp.float32)[None, :]
    base = jnp.exp(-jnp.abs(rows - cols) / (2.0 * CX))
    rough = jax.random.uniform(key, (NX, NX), jnp.float32, 0.5, 1.5)
    return (base * rough).astype(jnp.float32)


def with_ends(result, key, least, top_value):
    longest = result.shape.index(max(result.shape))
    spots = []
    for shift in (0, 1):
        where = [jax.random.randint(jax.random.fold_in(key, axis), (), 0, length) for axis, length in enumerate(result.shape)]
        where[longest] = (where[longest] + shift) % result.shape[longest]
        spots.append(tuple(where))
    return result.at[spots[0]].set(least).at[spots[1]].set(top_value)


def level_of(stream_key, dims, shards, least, largest):
    factor_of, own = 1.0, jax.random.fold_in(stream_key, 6)
    for dim, shards_of in shards:
        steps = jnp.exp(jax.random.uniform(jax.random.fold_in(own, dim), (shards_of,), jnp.float32, least / len(shards), largest / len(shards)))
        factor_of = factor_of * jnp.repeat(steps, dims[dim] // shards_of).reshape([-1 if axis == dim else 1 for axis in range(len(dims))])
    return factor_of


def shared_out(key, own, number, rows, count, top, reach, lean):
    sequence = jax.random.permutation(key, count)
    crowded, ordinary = load_shares(count, rows * top, reach, lean, True), load_shares(count, rows * top, reach, lean, False)
    places = jnp.arange(count)

    def named(lengths, offset_by):
        used = int((lengths > 0).sum())
        fixed = max(1, used // 4)
        shifted = fixed + (places - fixed + offset_by * (used - fixed)) % max(1, count - fixed)
        return jnp.zeros((count,), jnp.int32).at[sequence[jnp.where(places < fixed, places, shifted)]].set(jnp.asarray(lengths, jnp.int32))

    lengths = jnp.where(number % 4 == 0, named(crowded, number // 4), named(ordinary, number - number // 4 - 1))
    mixed = jax.random.permutation(jax.random.fold_in(own, 3), count)
    source_of, sink = mixed[0:count // 2 * 2:2], mixed[1:count // 2 * 2:2]
    room = jnp.minimum(lengths[source_of] - 1, reach - lengths[sink]) // 2
    room = jnp.where((source_of == sequence[0]) | (sink == sequence[0]) | (lengths[sink] == 0), 0, jnp.maximum(room, 0))
    shifted = jax.random.randint(jax.random.fold_in(own, 4), (count // 2,), 0, 1 << 20) % (room + 1)
    lengths = lengths.at[source_of].add(-shifted).at[sink].add(shifted)
    members = jnp.searchsorted(jnp.cumsum(lengths), jnp.arange(rows * top), side="right").astype(jnp.int32)
    listing = members.reshape(top, rows).T
    listing = listing[jax.random.permutation(jax.random.fold_in(own, 1), rows)]
    offset_by = jax.random.randint(jax.random.fold_in(own, 2), (rows, 1), 0, top)
    return jnp.take_along_axis(listing, (jnp.arange(top)[None, :] + offset_by) % top, axis=1)


def load_shares(amount, total, most, slope, full):
    weights = [(1 << 20) // math.isqrt(rank ** slope) + 1 for rank in range(1, amount + 1)]
    largest = most if full else min(most, max(-(-total // amount), total * weights[0] // sum(weights)))
    least = 1 if total - largest >= amount - 1 else 0
    given, surplus = [largest] + [least] * (amount - 1), total - largest - least * (amount - 1)
    while surplus > 0:
        movable = [i for i in range(1, amount) if given[i] < largest] or [i for i in range(1, amount) if given[i] < most]
        mass, left = sum([weights[i] for i in movable]), surplus
        for i in movable:
            addition = min(most - given[i], max(1, left * weights[i] // mass), surplus)
            given[i] = given[i] + addition
            surplus = surplus - addition
    return np.array(given)


def noise(rng, shape, scale, limit, shards=(), kind=jnp.bfloat16):
    drawn = jax.random.normal(rng, shape, jnp.float32) * scale
    if len(shards) > 0:
        drawn = level_of(rng, shape, shards, -0.22, 0.18) * drawn
    return jnp.clip(drawn, min=-limit, max=limit).astype(kind)


def setup_inputs(seed: int = 0) -> dict:
    key_list = jax.random.split(jax.random.key(seed), 8)
    model_state = noise(key_list[0], (3, NZ, NX, NY), 1.0, 6.0, ((2, 4), (3, 8)), jnp.float32)
    obs_val = noise(key_list[1], (RECS, 3 * OBS_LEV), 1.0, 6.0, ((0, 32),), jnp.float32)
    obs_owner_keys = jax.random.split(jax.random.fold_in(key_list[2], 1), RECS // REC_DEV)
    obs_owner_turns = jax.random.permutation(jax.random.fold_in(key_list[2], 3), RECS // REC_DEV)
    obs_owner = jax.vmap(lambda own, number: shared_out(jax.random.fold_in(key_list[2], 2), own, number, REC_DEV, N_GY, 1, CAPY, 2))(obs_owner_keys, obs_owner_turns).reshape((RECS, 1))
    obs_x = with_ends(jax.random.randint(key_list[3], (RECS,), 0, NX), jax.random.fold_in(key_list[3], 1), 0, NX - 1).astype(jnp.int32)
    obs_y = with_ends(jax.random.randint(key_list[4], (RECS,), 0, CY), jax.random.fold_in(key_list[4], 1), 0, CY - 1).astype(jnp.int32)
    cressman = draw_cressman(jax.random.fold_in(key_list[7], 71), 0)
    vertical = noise(key_list[6], (3, NZ, OBS_LEV), NZ ** -0.5, 2.0, (), jnp.float32)
    return dict(model_state=model_state, obs_val=obs_val, obs_owner=obs_owner, obs_x=obs_x, obs_y=obs_y, cressman=cressman, vertical=vertical)


advect_coef = 0.5
diffuse_h = 0.2
diffuse_z = 0.1
time_step = 0.5
nudge_gain = 1.0
spread_gain = 0.125


def tendency(padded):
    center = padded[:, :, 1:-1, 1:-1]
    to_east = padded[:, :, 2:, 1:-1]
    to_west = padded[:, :, :-2, 1:-1]
    to_north = padded[:, :, 1:-1, 2:]
    to_south = padded[:, :, 1:-1, :-2]
    wind_u = center[0][None]
    wind_v = center[1][None]
    advection = -0.5 * advect_coef * (wind_u * (to_east - to_west) + wind_v * (to_north - to_south))
    laplace = to_east + to_west + to_north + to_south - 4.0 * center
    upper_cells = jnp.concatenate([center[:, 1:], center[:, -1:]], axis=1)
    lower_cells = jnp.concatenate([center[:, :1], center[:, :-1]], axis=1)
    return advection + diffuse_h * laplace + diffuse_z * (upper_cells + lower_cells - 2.0 * center)


def reference(model_state, obs_val, obs_owner, obs_x, obs_y, cressman, vertical):
    fields, levels, width_x, width_y = model_state.shape
    obs_levels = vertical.shape[2]
    records = obs_val.shape[0]
    block = math.gcd(records, 512)
    blocks = records // block
    columns = (obs_owner[:, 0] * CY + obs_y).astype(jnp.int32)
    highest = lax.Precision.HIGHEST

    def per_block(running, piece):
        numer, weights_sum = running
        x_cells, y_cells, values = piece
        weight = jnp.take(cressman, x_cells, axis=0)
        picked = jnp.take(model_state, y_cells, axis=3)
        colsum = jnp.einsum('vzxb,bx->bvz', picked, weight, precision=highest)
        total = jnp.sum(weight, axis=1)
        model_eq = jnp.einsum('bvz,vzl->bvl', colsum / total[:, None, None], vertical, precision=highest)
        innovation = values - model_eq
        spread = jnp.einsum('bvl,vzl->bvz', innovation, vertical, precision=highest) * spread_gain
        weighted = spread[:, :, :, None] * weight[:, None, None, :]
        numer = numer.at[y_cells].add(weighted)
        weights_sum = weights_sum.at[y_cells].add(weight)
        return (numer, weights_sum), None

    start = (jnp.zeros((width_y, fields, levels, width_x), jnp.float32), jnp.zeros((width_y, width_x), jnp.float32))
    pieces = (obs_x.reshape(blocks, block), columns.reshape(blocks, block), obs_val.reshape(blocks, block, fields, obs_levels))
    (numer, weights_sum), _ = lax.scan(per_block, start, pieces)
    nudge = jnp.transpose(numer, (1, 2, 3, 0)) / jnp.maximum(jnp.transpose(weights_sum), 1.0)[None, None]
    padded = jnp.pad(model_state, ((0, 0), (0, 0), (1, 1), (1, 1)))
    return model_state + time_step * (tendency(padded) + nudge_gain * nudge)
```

```python
import functools

import jax
import jax.numpy as jnp
from jax import lax
from jax.experimental import pallas as pl
from jax.experimental.pallas import tpu as pltpu
from jax.sharding import PartitionSpec as P

advect_coef = 0.5
diffuse_h = 0.2
diffuse_z = 0.1
time_step = 0.5
nudge_gain = 1.0
spread_gain = 0.125

LANES = 128
WORDS = 32
LANE_STEP = 32
YB = 16
RB = 256
VMEM_LIMIT = 48 * 1024 * 1024

HIGHEST = lax.Precision.HIGHEST
NT = (((1,), (1,)), ((), ()))
NN = (((1,), (0,)), ((), ()))
VMEM = pl.BlockSpec(memory_space=pltpu.VMEM)
ANY = pl.BlockSpec(memory_space=pl.ANY)
SMEM = pl.BlockSpec(memory_space=pltpu.SMEM)


def dot(a, b, dims=NN, precision=None):
    return lax.dot_general(a, b, dims, precision=precision, preferred_element_type=jnp.float32)


def split2(value):
    high = value.astype(jnp.bfloat16)
    low = (value - high.astype(jnp.float32)).astype(jnp.bfloat16)
    return high, low


def iota(shape, axis):
    return lax.broadcasted_iota(jnp.int32, shape, axis)


def pack_kernel(count_y, cap, owner_ref, x_ref, y_ref, obs_ref, vert_ref, msg_ref, gram_ref):
    records = x_ref.shape[1]
    kinds = vert_ref.shape[0]
    levels = kinds // 3
    vert = vert_ref[...]
    terms = []
    for v in range(3):
        obs = obs_ref[:, v * LANES : (v + 1) * LANES]
        terms.append(dot(vert[v * levels : (v + 1) * levels], obs, NT, HIGHEST) * spread_gain)
    row = iota((8, records), 0)
    x_row = jnp.broadcast_to(x_ref[...].astype(jnp.float32), (8, records))
    y_row = jnp.broadcast_to(y_ref[...].astype(jnp.float32) - float(LANES), (8, records))
    head = jnp.where(row == 0, x_row, jnp.where(row == 1, y_row, 0.0))
    payload = jnp.concatenate([head] + terms, axis=0)

    owner = owner_ref[...].astype(jnp.float32)
    owner_lanes = jnp.broadcast_to(owner, (records, records))
    owner_rows = jnp.transpose(owner_lanes)
    earlier = iota((records, records), 0) < iota((records, records), 1)
    same = jnp.where((owner_lanes == owner_rows) & earlier, 1.0, 0.0)
    rank = jnp.sum(same, axis=0, keepdims=True)
    slot = owner * float(cap) + rank
    places = count_y * cap
    pick = jnp.where(iota((places, records), 0).astype(jnp.float32) == slot, 1.0, 0.0)
    out = dot(payload, pick, NT, HIGHEST)

    lane = iota((8, LANES), 1)
    for c in range(count_y):
        chunk = (c * cap) // LANES
        offset = (c * cap) % LANES
        block = jnp.zeros((8, LANES), jnp.float32)
        for j in range(WORDS // 8):
            part = out[8 * j : 8 * j + 8, chunk * LANES : (chunk + 1) * LANES]
            shift = (LANE_STEP * j - offset) % LANES
            if shift:
                part = pltpu.roll(part, shift, 1)
            inside = (lane >= LANE_STEP * j) & (lane < LANE_STEP * j + cap)
            block = jnp.where(inside, part, block)
        for g in range(msg_ref.shape[0] // count_y):
            msg_ref[g * count_y + c] = block

    gram = dot(vert, vert, NT, HIGHEST) * spread_gain
    alike = (iota((kinds, kinds), 0) // levels) == (iota((kinds, kinds), 1) // levels)
    gram_ref[...] = jnp.where(alike, gram, 0.0)


def turn_kernel(planes, state_ref, cress_ref, hi_ref, lo_ref, ct_hi_ref, ct_lo_ref, first_y_ref, last_y_ref, first_x_ref, last_x_ref):
    step = pl.program_id(0)
    for p in range(planes):
        k = step * planes + p
        plane = state_ref[p]
        turned = jnp.transpose(plane)
        high, low = split2(turned)
        hi_ref[p] = high
        lo_ref[p] = low
        first_y_ref[pl.ds(k, 1), :] = turned[0:1]
        last_y_ref[pl.ds(k, 1), :] = turned[turned.shape[0] - 1 :]
        first_x_ref[pl.ds(k, 1), :] = plane[0:1]
        last_x_ref[pl.ds(k, 1), :] = plane[plane.shape[0] - 1 :]
    high, low = split2(jnp.transpose(cress_ref[...]))
    ct_hi_ref[...] = high
    ct_lo_ref[...] = low


def unpack(recv_ref, cap, j):
    devices = recv_ref.shape[0]
    per = LANES // cap
    lane = iota((8, LANES), 1)
    chunks = []
    for q in range(devices // per):
        block = jnp.zeros((8, LANES), jnp.float32)
        for t in range(per):
            part = recv_ref[q * per + t]
            shift = (cap * t - LANE_STEP * j) % LANES
            if shift:
                part = pltpu.roll(part, shift, 1)
            inside = (lane >= cap * t) & (lane < cap * t + cap)
            block = jnp.where(inside, part, block)
        chunks.append(block)
    return chunks


def edge_place(slots, k, side):
    per = slots // LANES
    rows = -(-24 // per)
    return 25 + side * rows + k // per, (k % per) * LANES


def sums_kernel(
    cap, tile_y, recv_ref, first_x_ref, last_x_ref, mt_hi_hbm, mt_lo_hbm, ct_hi_hbm, ct_lo_hbm,
    msg_ref, wt_hi_ref, wt_lo_ref, ys_ref, terms_ref, bounds_ref,
    mt_hi, mt_lo, ct_hi, ct_lo, rank_ref, acc_ref, sems,
):
    copies = [
        pltpu.make_async_copy(src, dst, sems.at[i])
        for i, (src, dst) in enumerate(
            ((ct_hi_hbm, ct_hi), (ct_lo_hbm, ct_lo), (mt_hi_hbm, mt_hi), (mt_lo_hbm, mt_lo))
        )
    ]
    for copy in copies:
        copy.start()
    slots = recv_ref.shape[0] * cap
    chunks = slots // LANES
    kinds, _, tile_x = mt_hi.shape
    width = ct_hi.shape[1]

    groups = [unpack(recv_ref, cap, j) for j in range(WORDS // 8)]
    keys = []
    for c in range(chunks):
        place = (iota((1, LANES), 1) + c * LANES).astype(jnp.float32)
        keys.append((groups[0][c][1:2] + float(tile_y)) * float(slots) + place)
    counts = [jnp.zeros((8, LANES), jnp.float32) for _ in range(chunks)]
    for c in range(chunks):
        column = jnp.transpose(jnp.broadcast_to(keys[c], (LANES, LANES)))
        for d in range(chunks):
            less = jnp.where(column < keys[d], 1.0, 0.0)
            counts[d] = counts[d] + jnp.sum(less.reshape(LANES // 8, 8, LANES), axis=0)
    rank = jnp.concatenate([jnp.sum(count, axis=0, keepdims=True) for count in counts], axis=1)

    rows = []
    head = jnp.concatenate(groups[0], axis=1)
    x_high = jnp.floor(head[0:1] * 0.125)
    row = iota((8, slots), 0)
    top = jnp.where(
        row == 0,
        jnp.broadcast_to(x_high, (8, slots)),
        jnp.where(
            row == 1,
            jnp.broadcast_to(head[0:1] - 8.0 * x_high, (8, slots)),
            jnp.where(row == 2, jnp.broadcast_to(head[1:2] + float(tile_y), (8, slots)), 0.0),
        ),
    )
    words = jnp.concatenate([jnp.concatenate(group, axis=1) for group in groups[1:]], axis=0)
    high = words.astype(jnp.bfloat16).astype(jnp.float32)
    middle = (words - high).astype(jnp.bfloat16).astype(jnp.float32)
    low = words - high - middle
    table = jnp.concatenate([top, high, middle, low], axis=0).astype(jnp.bfloat16)

    for copy in copies[:2]:
        copy.wait()
    blocks = slots // RB
    for j in range(blocks):
        lanes = slice(j * RB, (j + 1) * RB)
        place = (iota((RB, slots), 0) + j * RB).astype(jnp.float32)
        pick = jnp.where(place == rank, 1.0, 0.0).astype(jnp.bfloat16)
        ordered = dot(table, pick, NT)
        xs = ordered[0:1] * 8.0 + ordered[1:2]
        ys = ordered[2:3]
        ys_ref[:, lanes] = jnp.broadcast_to(ys, (8, RB))
        terms_ref[:, lanes] = ordered[8:32] + ordered[32:56] + ordered[56:80]
        hot = jnp.where(iota((width, RB), 0).astype(jnp.float32) == xs, 1.0, 0.0)
        hot = hot.astype(jnp.bfloat16)
        wt_hi_ref[:, lanes] = dot(ct_hi[...], hot).astype(jnp.bfloat16)
        wt_lo_ref[:, lanes] = dot(ct_lo[...], hot).astype(jnp.bfloat16)
        least = jnp.min(ys).astype(jnp.int32)
        most = jnp.minimum(jnp.max(ys).astype(jnp.int32), tile_y - 1)
        bounds_ref[2 * j] = least // YB
        bounds_ref[2 * j + 1] = most // YB + 1

    for copy in copies[2:]:
        copy.wait()
    ones = jnp.ones((8, tile_x), jnp.bfloat16)
    for j in range(blocks):
        lanes = slice(j * RB, (j + 1) * RB)
        acc_ref[...] = jnp.zeros_like(acc_ref)

        def add_pair(b, carry, lanes=lanes):
            start = pl.multiple_of(b * YB, YB)
            a_hi = mt_hi[:, pl.ds(start, YB), :].reshape(kinds * YB, tile_x)
            a_lo = mt_lo[:, pl.ds(start, YB), :].reshape(kinds * YB, tile_x)
            w_hi, w_lo = wt_hi_ref[:, lanes], wt_lo_ref[:, lanes]
            part = dot(a_hi, w_hi) + dot(a_hi, w_lo) + dot(a_lo, w_hi)
            named = (iota((YB, RB), 0) + start).astype(jnp.float32) == ys_ref[0:1, lanes]
            kept = jnp.where(named[None], part.reshape(kinds, YB, RB), 0.0)
            acc_ref[...] += kept[:, :8] + kept[:, 8:]
            return carry

        lax.fori_loop(bounds_ref[2 * j], bounds_ref[2 * j + 1], add_pair, 0)
        msg_ref[0:kinds, lanes] = jnp.sum(acc_ref[...], axis=1)
        total = dot(ones, wt_hi_ref[:, lanes]) + dot(ones, wt_lo_ref[:, lanes])
        msg_ref[kinds : kinds + 1, lanes] = total[0:1]
    msg_ref[kinds + 1 :, :] = jnp.zeros((WORDS - kinds - 1, slots), jnp.float32)
    for side, edge_ref in enumerate((first_x_ref, last_x_ref)):
        for k in range(kinds):
            r, at = edge_place(slots, k, side)
            msg_ref[r : r + 1, at : at + LANES] = edge_ref[k : k + 1, :]


def stencil_kernel(state_hbm, out_hbm, state, out, in_sems, out_sems):
    fields, levels, tile_x, tile_y = state.shape
    reads = [
        pltpu.make_async_copy(state_hbm.at[:, z], state.at[:, z], in_sems.at[z])
        for z in range(levels)
    ]
    writes = [
        pltpu.make_async_copy(out.at[:, z], out_hbm.at[:, z], out_sems.at[z])
        for z in range(levels)
    ]
    for read in reads:
        read.start()
    reads[0].wait()
    row = iota((tile_x, tile_y), 0)
    lane = iota((tile_x, tile_y), 1)
    wind = 0.5 * time_step * advect_coef
    across = time_step * diffuse_h
    upward = time_step * diffuse_z
    keep = 1.0 - 4.0 * across - 2.0 * upward
    for z in range(levels):
        if z + 1 < levels:
            reads[z + 1].wait()
        u = wind * state[0, z]
        v = wind * state[1, z]
        east_gain = jnp.where(row == tile_x - 1, 0.0, across - u)
        west_gain = jnp.where(row == 0, 0.0, across + u)
        north_gain = jnp.where(lane == tile_y - 1, 0.0, across - v)
        south_gain = jnp.where(lane == 0, 0.0, across + v)
        for f in range(fields):
            cell = state[f, z]
            stacked = state[f, min(z + 1, levels - 1)] + state[f, max(z - 1, 0)]
            total = keep * cell + upward * stacked
            total = total + east_gain * pltpu.roll(cell, tile_x - 1, 0)
            total = total + west_gain * pltpu.roll(cell, 1, 0)
            total = total + north_gain * pltpu.roll(cell, tile_y - 1, 1)
            total = total + south_gain * pltpu.roll(cell, 1, 1)
            out[f, z] = total
        writes[z].start()
    for write in writes:
        write.wait()


def nudge_kernel(
    stages, flags_ref, bounds_ref, *refs
):
    sum_ref, recv_refs, refs = refs[0], refs[1 : 1 + stages], refs[1 + stages :]
    (terms_ref, gram_ref, ys_ref, wt_hi_ref, wt_lo_ref, own_first, own_last, south_ref, north_ref,
     base_hbm, out_hbm, num_ref, base, spread_ref, in_sem, out_sems) = refs
    kinds, tile_x, tile_y = base.shape
    levels = kinds // 3
    slots = ys_ref.shape[1]
    blocks = slots // RB
    read = pltpu.make_async_copy(base_hbm, base, in_sem)
    read.start()
    num_ref[...] = jnp.zeros_like(num_ref)
    total = sum_ref[0 : kinds + 1, :] + recv_refs[-1][0 : kinds + 1, :]
    averaged = total[0:kinds] / total[kinds : kinds + 1]
    spread_ref[0:kinds, :] = terms_ref[...] - dot(gram_ref[...], averaged, NN, HIGHEST)
    spread_ref[kinds : kinds + 1, :] = jnp.ones((1, slots), jnp.float32)

    for j in range(blocks):
        lanes = slice(j * RB, (j + 1) * RB)

        def add_pair(b, carry, lanes=lanes):
            start = pl.multiple_of(b * YB, YB)
            named = (iota((YB, RB), 0) + start).astype(jnp.float32) == ys_ref[0:1, lanes]
            spread = spread_ref[0 : kinds + 1, lanes]
            placed = jnp.where(named[None], spread[:, None, :], 0.0)
            b_hi, b_lo = split2(placed.reshape((kinds + 1) * YB, RB))
            w_hi, w_lo = wt_hi_ref[:, lanes], wt_lo_ref[:, lanes]
            part = dot(b_hi, w_hi, NT) + dot(b_hi, w_lo, NT) + dot(b_lo, w_hi, NT)
            num_ref[:, pl.ds(start, YB), :] += part.reshape(kinds + 1, YB, tile_x)
            return carry

        lax.fori_loop(bounds_ref[2 * j], bounds_ref[2 * j + 1], add_pair, 0)

    wind = 0.5 * time_step * advect_coef
    across = time_step * diffuse_h
    scale = time_step * nudge_gain / jnp.maximum(num_ref[kinds], 1.0)
    read.wait()
    for k in range(kinds):
        z = k % levels
        turned = num_ref[k] * scale
        south = south_ref[k : k + 1, :] * (across + wind * own_first[levels + z : levels + z + 1, :])
        north = north_ref[k : k + 1, :] * (across - wind * own_last[levels + z : levels + z + 1, :])
        cell_row = iota(turned.shape, 0)
        turned = turned + jnp.where(
            cell_row == 0, south, jnp.where(cell_row == tile_y - 1, north, 0.0)
        )
        base[k] = base[k] + jnp.transpose(turned)
        west = jnp.zeros((1, tile_y), jnp.float32)
        east = jnp.zeros((1, tile_y), jnp.float32)
        for s in range(stages):
            r, at = edge_place(slots, k, 1)
            west = west + jnp.where(flags_ref[2 * s] == 1, recv_refs[s][r : r + 1, at : at + LANES], 0.0)
            r, at = edge_place(slots, k, 0)
            east = east + jnp.where(flags_ref[2 * s + 1] == 1, recv_refs[s][r : r + 1, at : at + LANES], 0.0)
        r, at = edge_place(slots, z, 0)
        u_first = sum_ref[r : r + 1, at : at + LANES]
        r, at = edge_place(slots, z, 1)
        u_last = sum_ref[r : r + 1, at : at + LANES]
        base[k, 0:1, :] += west * (across + wind * u_first)
        base[k, tile_x - 1 : tile_x, :] += east * (across - wind * u_last)
        pltpu.make_async_copy(base.at[k], out_hbm.at[k], out_sems.at[k]).start()
    for k in range(kinds):
        pltpu.make_async_copy(base.at[k], out_hbm.at[k], out_sems.at[k]).wait()


def call(kernel, name, out_shape, in_specs, out_specs, scratch=(), flops=0, moved=0, **kwargs):
    return pl.pallas_call(
        kernel,
        name=name,
        out_shape=out_shape,
        in_specs=in_specs,
        out_specs=out_specs,
        scratch_shapes=list(scratch),
        compiler_params=pltpu.CompilerParams(vmem_limit_bytes=VMEM_LIMIT),
        cost_estimate=pl.CostEstimate(flops=flops, bytes_accessed=moved, transcendentals=0),
        **kwargs,
    )


def local(model_state, obs_val, obs_owner, obs_x, obs_y, cressman, vertical):
    count_x = lax.axis_size("gx")
    count_y = lax.axis_size("gy")
    fields, levels, tile_x, tile_y = model_state.shape
    kinds = fields * levels
    records = obs_val.shape[0]
    width = cressman.shape[0]
    cap = max(2, 2 * records // count_y)
    slots = count_x * count_y * cap
    blocks = slots // RB
    f32, bf16, i32 = jnp.float32, jnp.bfloat16, jnp.int32
    shape = jax.ShapeDtypeStruct
    stages = count_x.bit_length() - 1

    msg, gram = call(
        functools.partial(pack_kernel, count_y, cap),
        "pack_records",
        (shape((count_x * count_y, 8, LANES), f32), shape((kinds, kinds), f32)),
        [VMEM] * 5,
        (VMEM, VMEM),
        flops=10**7,
        moved=10**6,
    )(
        obs_owner.reshape(1, records),
        obs_x.reshape(1, records),
        obs_y.reshape(1, records),
        obs_val,
        vertical.reshape(kinds, vertical.shape[2]),
    )
    recv = lax.all_to_all(msg, ("gx", "gy"), split_axis=0, concat_axis=0, tiled=True)

    steps = 12
    planes, piece = kinds // steps, width // steps
    whole = lambda *dims: pl.BlockSpec(dims, lambda i: (0,) * len(dims))
    state3 = model_state.reshape(kinds, tile_x, tile_y)
    mt_hi, mt_lo, ct_hi, ct_lo, first_y, last_y, first_x, last_x = call(
        functools.partial(turn_kernel, planes),
        "turn_state",
        (
            shape((kinds, tile_y, tile_x), bf16),
            shape((kinds, tile_y, tile_x), bf16),
            shape((tile_x, width), bf16),
            shape((tile_x, width), bf16),
            shape((kinds, tile_x), f32),
            shape((kinds, tile_x), f32),
            shape((kinds, tile_y), f32),
            shape((kinds, tile_y), f32),
        ),
        [
            pl.BlockSpec((planes, tile_x, tile_y), lambda i: (i, 0, 0)),
            pl.BlockSpec((piece, tile_x), lambda i: (i, 0)),
        ],
        (
            pl.BlockSpec((planes, tile_y, tile_x), lambda i: (i, 0, 0)),
            pl.BlockSpec((planes, tile_y, tile_x), lambda i: (i, 0, 0)),
            pl.BlockSpec((tile_x, piece), lambda i: (0, i)),
            pl.BlockSpec((tile_x, piece), lambda i: (0, i)),
            whole(kinds, tile_x),
            whole(kinds, tile_x),
            whole(kinds, tile_y),
            whole(kinds, tile_y),
        ),
        grid=(steps,),
        moved=15 * 10**6,
    )(state3, cressman)

    up = [(i, i + 1) for i in range(count_y - 1)]
    down = [(i + 1, i) for i in range(count_y - 1)]
    south = lax.ppermute(last_y, "gy", up)
    north = lax.ppermute(first_y, "gy", down)

    partial, wt_hi, wt_lo, ys, terms, bounds = call(
        functools.partial(sums_kernel, cap, tile_y),
        "column_sums",
        (
            shape((WORDS, slots), f32),
            shape((tile_x, slots), bf16),
            shape((tile_x, slots), bf16),
            shape((8, slots), f32),
            shape((kinds, slots), f32),
            shape((2 * blocks,), i32),
        ),
        [VMEM] * 3 + [ANY] * 4,
        (VMEM, VMEM, VMEM, VMEM, VMEM, SMEM),
        [
            pltpu.VMEM((kinds, tile_y, tile_x), bf16),
            pltpu.VMEM((kinds, tile_y, tile_x), bf16),
            pltpu.VMEM((tile_x, width), bf16),
            pltpu.VMEM((tile_x, width), bf16),
            pltpu.VMEM((8, slots), f32),
            pltpu.VMEM((kinds, 8, RB), f32),
            pltpu.SemaphoreType.DMA((4,)),
        ],
        flops=4 * 10**9,
        moved=10**7,
    )(recv, first_x, last_x, mt_hi, mt_lo, ct_hi, ct_lo)

    summed, received = partial, []
    summing = (jnp.arange(WORDS) < kinds + 1)[:, None]
    for s in range(stages):
        mask = 2 ** (s + 1) - 1
        got = lax.ppermute(summed, "gx", [(i, i ^ mask) for i in range(count_x)])
        received.append(got)
        if s < stages - 1:
            summed = jnp.where(summing, summed + got, summed)

    base = call(
        stencil_kernel,
        "stencil",
        shape(model_state.shape, f32),
        [ANY],
        ANY,
        [
            pltpu.VMEM(model_state.shape, f32),
            pltpu.VMEM(model_state.shape, f32),
            pltpu.SemaphoreType.DMA((levels,)),
            pltpu.SemaphoreType.DMA((levels,)),
        ],
        moved=10**7,
    )(model_state)

    me = lax.axis_index("gx")
    flags = []
    for s in range(stages):
        partner = me ^ (2 ** (s + 1) - 1)
        flags += [partner == me - 1, partner == me + 1]
    flags = jnp.stack(flags).astype(i32)

    out = call(
        functools.partial(nudge_kernel, stages),
        "nudge",
        shape((kinds, tile_x, tile_y), f32),
        [SMEM, SMEM] + [VMEM] * (10 + stages) + [ANY],
        ANY,
        [
            pltpu.VMEM((kinds + 1, tile_y, tile_x), f32),
            pltpu.VMEM((kinds, tile_x, tile_y), f32),
            pltpu.VMEM((WORDS, slots), f32),
            pltpu.SemaphoreType.DMA,
            pltpu.SemaphoreType.DMA((kinds,)),
        ],
        flops=4 * 10**9,
        moved=10**7,
    )(
        flags, bounds, summed, *received, terms, gram, ys, wt_hi, wt_lo,
        first_y, last_y, south, north, base.reshape(kinds, tile_x, tile_y),
    )
    return out.reshape(model_state.shape)


def solution(mesh):
    in_specs = (
        P(None, None, "gx", "gy"),
        P(("gx", "gy"), None),
        P(("gx", "gy"), None),
        P(("gx", "gy")),
        P(("gx", "gy")),
        P(None, "gx"),
        P(),
    )
    out_specs = P(None, None, "gx", "gy")
    return jax.shard_map(local, mesh=mesh, in_specs=in_specs, out_specs=out_specs, check_vma=False)
```

```python
import functools

import jax
import jax.numpy as jnp
from jax import lax
from jax.experimental import pallas as pl
from jax.experimental.pallas import tpu as pltpu
from jax.sharding import PartitionSpec as P

advect_coef = 0.5
diffuse_h = 0.2
diffuse_z = 0.1
time_step = 0.5
nudge_gain = 1.0
spread_gain = 0.125

LANES = 128
WORDS = 32
LANE_STEP = 32
YB = 16
RB = 256
MIB = 1024 * 1024
MOST = 58
SOME = 50

HIGHEST = lax.Precision.HIGHEST
NT = (((1,), (1,)), ((), ()))
NN = (((1,), (0,)), ((), ()))
VMEM = pl.BlockSpec(memory_space=pltpu.VMEM)
ANY = pl.BlockSpec(memory_space=pl.ANY)
SMEM = pl.BlockSpec(memory_space=pltpu.SMEM)
HBM = pl.BlockSpec(memory_space=pltpu.HBM)


def dot(a, b, dims=NN, precision=None):
    return lax.dot_general(a, b, dims, precision=precision, preferred_element_type=jnp.float32)


def split2(value):
    high = value.astype(jnp.bfloat16)
    low = (value - high.astype(jnp.float32)).astype(jnp.bfloat16)
    return high, low


def iota(shape, axis):
    return lax.broadcasted_iota(jnp.int32, shape, axis)


def pack_kernel(count_y, cap, *refs):
    sources, (msg_ref, gram_ref), places, sems = refs[:5], refs[5:7], refs[7:12], refs[12]
    copies = [pltpu.make_async_copy(a, b, sems.at[i]) for i, (a, b) in enumerate(zip(sources, places))]
    for copy in copies:
        copy.start()
    for copy in copies:
        copy.wait()
    owner_ref, x_ref, y_ref, obs_ref, vert_ref = places
    records, kinds = x_ref.shape[1], vert_ref.shape[0]
    levels = kinds // 3
    vert = vert_ref[...]
    terms = []
    for v in range(3):
        obs = obs_ref[:, v * LANES : (v + 1) * LANES]
        terms.append(dot(vert[v * levels : (v + 1) * levels], obs, NT, HIGHEST) * spread_gain)
    row = iota((8, records), 0)
    x_row = jnp.broadcast_to(x_ref[...].astype(jnp.float32), (8, records))
    y_row = jnp.broadcast_to(y_ref[...].astype(jnp.float32) - float(LANES), (8, records))
    head = jnp.where(row == 0, x_row, jnp.where(row == 1, y_row, 0.0))
    payload = jnp.concatenate([head] + terms, axis=0)

    owner = owner_ref[...].astype(jnp.float32)
    owner_lanes = jnp.broadcast_to(owner, (records, records))
    owner_rows = jnp.transpose(owner_lanes)
    earlier = iota((records, records), 0) < iota((records, records), 1)
    same = jnp.where((owner_lanes == owner_rows) & earlier, 1.0, 0.0)
    rank = jnp.sum(same, axis=0, keepdims=True)
    slot = owner * float(cap) + rank
    places = count_y * cap
    pick = jnp.where(iota((places, records), 0).astype(jnp.float32) == slot, 1.0, 0.0)
    out = dot(payload, pick, NT, HIGHEST)

    lane = iota((8, LANES), 1)
    for c in range(count_y):
        chunk = (c * cap) // LANES
        offset = (c * cap) % LANES
        block = jnp.zeros((8, LANES), jnp.float32)
        for j in range(WORDS // 8):
            part = out[8 * j : 8 * j + 8, chunk * LANES : (chunk + 1) * LANES]
            shift = (LANE_STEP * j - offset) % LANES
            if shift:
                part = pltpu.roll(part, shift, 1)
            inside = (lane >= LANE_STEP * j) & (lane < LANE_STEP * j + cap)
            block = jnp.where(inside, part, block)
        for g in range(msg_ref.shape[0] // count_y):
            msg_ref[g * count_y + c] = block

    gram = dot(vert, vert, NT, HIGHEST) * spread_gain
    alike = (iota((kinds, kinds), 0) // levels) == (iota((kinds, kinds), 1) // levels)
    gram_ref[...] = jnp.where(alike, gram, 0.0)


def unpack(recv_ref, cap, j):
    devices = recv_ref.shape[0]
    per = LANES // cap
    lane = iota((8, LANES), 1)
    chunks = []
    for q in range(devices // per):
        block = jnp.zeros((8, LANES), jnp.float32)
        for t in range(per):
            part = recv_ref[q * per + t]
            shift = (cap * t - LANE_STEP * j) % LANES
            if shift:
                part = pltpu.roll(part, shift, 1)
            inside = (lane >= cap * t) & (lane < cap * t + cap)
            block = jnp.where(inside, part, block)
        chunks.append(block)
    return chunks


def pair_list(bounds_ref, blocks, y_blocks):
    j, b = jnp.int32(0), bounds_ref[0]
    pairs = []
    for _ in range(blocks + y_blocks - 1):
        valid = (j < blocks) & (b < bounds_ref[2 * jnp.minimum(j, blocks - 1) + 1])
        pairs.append((jnp.minimum(j, blocks - 1), jnp.where(valid, b, y_blocks + 1)))
        more = b + 1 < bounds_ref[2 * jnp.minimum(j, blocks - 1) + 1]
        following = jnp.minimum(j + 1, blocks - 1)
        b = jnp.where(more, b + 1, bounds_ref[2 * following])
        j = jnp.where(more, j, jnp.minimum(j + 1, blocks))
    return pairs


def edge_place(slots, k, side):
    per = slots // LANES
    rows = -(-24 // per)
    return 25 + side * rows + k // per, (k % per) * LANES


def sums_kernel(
    cap, recv_ref, edge_hbm, state_hbm, cress_hbm,
    msg_ref, wt_ref, ys_ref, terms_ref, bounds_ref, give_a_ref, give_b_ref,
    acc_ref, edge_ref, state, cress, mt_hi, mt_lo, ct, sems, edge_sem,
):
    kinds, tile_x, tile_y = state.shape
    width = cress.shape[0]
    blocks = recv_ref.shape[0] * cap // RB
    piece, planes = width // blocks, kinds // blocks
    cress_reads, state_reads = [], []
    for i in range(blocks):
        rows, some = pl.ds(i * piece, piece), pl.ds(i * planes, planes)
        cress_reads.append(pltpu.make_async_copy(cress_hbm.at[rows], cress.at[rows], sems.at[i]))
        state_reads.append(pltpu.make_async_copy(state_hbm.at[some], state.at[some], sems.at[blocks + i]))
    for read in cress_reads:
        read.start()
    slots = recv_ref.shape[0] * cap
    chunks = slots // LANES

    groups = [unpack(recv_ref, cap, j) for j in range(WORDS // 8)]
    keys = []
    for c in range(chunks):
        place = (iota((1, LANES), 1) + c * LANES).astype(jnp.float32)
        keys.append((groups[0][c][1:2] + float(tile_y)) * float(slots) + place)
    counts = [jnp.zeros((8, LANES), jnp.float32) for _ in range(chunks)]
    for c in range(chunks):
        column = jnp.transpose(jnp.broadcast_to(keys[c], (LANES, LANES)))
        for d in range(chunks):
            less = jnp.where(column < keys[d], 1.0, 0.0)
            counts[d] = counts[d] + jnp.sum(less.reshape(LANES // 8, 8, LANES), axis=0)
    rank = jnp.concatenate([jnp.sum(count, axis=0, keepdims=True) for count in counts], axis=1)

    rows = []
    head = jnp.concatenate(groups[0], axis=1)
    x_high = jnp.floor(head[0:1] * 0.0625)
    row = iota((8, slots), 0)
    top = jnp.where(
        row == 0,
        jnp.broadcast_to(x_high, (8, slots)),
        jnp.where(
            row == 1,
            jnp.broadcast_to(head[0:1] - 16.0 * x_high, (8, slots)),
            jnp.where(row == 2, jnp.broadcast_to(head[1:2] + float(tile_y), (8, slots)), 0.0),
        ),
    )
    words = jnp.concatenate([jnp.concatenate(group, axis=1) for group in groups[1:]], axis=0)
    high = words.astype(jnp.bfloat16).astype(jnp.float32)
    middle = (words - high).astype(jnp.bfloat16).astype(jnp.float32)
    low = words - high - middle
    table = jnp.concatenate([top, high, middle, low], axis=0).astype(jnp.bfloat16)

    for read in state_reads:
        read.start()
    even = lax.rem(lax.axis_index("gy"), 2) == 0
    edge_read = pltpu.make_async_copy(edge_hbm, edge_ref, edge_sem)
    edge_read.start()
    x_rows = []
    for j in range(blocks):
        lanes = slice(j * RB, (j + 1) * RB)
        place = (iota((RB, slots), 0) + j * RB).astype(jnp.float32)
        pick = jnp.where(place == rank, 1.0, 0.0).astype(jnp.bfloat16)
        ordered = dot(table, pick, NT)
        x_rows.append(ordered[0:1] * 16.0 + ordered[1:2])
        ys = ordered[2:3]
        ys_ref[:, lanes] = jnp.broadcast_to(ys, (8, RB))
        terms_ref[:, lanes] = ordered[8:32] + ordered[32:56] + ordered[56:80]
        least = jnp.min(ys).astype(jnp.int32)
        most = jnp.minimum(jnp.max(ys).astype(jnp.int32), tile_y - 1)
        bounds_ref[2 * j] = least // YB
        bounds_ref[2 * j + 1] = most // YB + 1

    for read in cress_reads:
        read.wait()
    for i in range(width // LANES):
        rows = slice(i * LANES, (i + 1) * LANES)
        high, low = split2(jnp.transpose(cress[rows, :]))
        ct[0:tile_x, rows] = high
        ct[tile_x:, rows] = low

    def gather(j):
        hot = jnp.where(iota((width, RB), 0).astype(jnp.float32) == x_rows[j], 1.0, 0.0)
        wt = dot(ct[...], hot.astype(jnp.bfloat16))
        wt_ref[:, j * RB : (j + 1) * RB] = wt.astype(jnp.bfloat16)

    half = blocks // 2
    for j in range(half):
        gather(j)
    for read in state_reads:
        read.wait()
    planes = kinds // (blocks - half)
    for j in range(half, blocks):
        gather(j)
        for k in range((j - half) * planes, (j - half + 1) * planes):
            turned = jnp.transpose(state[k])
            high, low = split2(turned)
            mt_hi[k] = high
            mt_lo[k] = low
            first, last = turned[0:1], turned[tile_y - 1 :]
            give_a_ref[k : k + 1, :] = jnp.where(even, last, first)
            give_b_ref[k : k + 1, :] = jnp.where(even, first, last)

    acc_ref[...] = jnp.zeros_like(acc_ref)
    y_blocks = tile_y // YB
    for j, b in pair_list(bounds_ref, blocks, y_blocks):
        lanes = pl.ds(pl.multiple_of(j * RB, RB), RB)
        start = pl.multiple_of(jnp.minimum(b, y_blocks - 1) * YB, YB)
        a_hi = mt_hi[:, pl.ds(start, YB), :].reshape(kinds * YB, tile_x)
        a_lo = mt_lo[:, pl.ds(start, YB), :].reshape(kinds * YB, tile_x)
        w_hi = wt_ref[0:tile_x, lanes]
        part = dot(jnp.concatenate([a_hi, a_hi], axis=1), wt_ref[:, lanes]) + dot(a_lo, w_hi)
        named = (iota((YB, RB), 0) + b * YB).astype(jnp.float32) == ys_ref[0:1, lanes]
        kept = jnp.where(named[None], part.reshape(kinds, YB, RB), 0.0)
        acc_ref[j] += kept[:, :8] + kept[:, 8:]

    ones = jnp.ones((8, 2 * tile_x), jnp.bfloat16)
    for j in range(blocks):
        lanes = slice(j * RB, (j + 1) * RB)
        msg_ref[0:kinds, lanes] = jnp.sum(acc_ref[j], axis=1)
        total = dot(ones, wt_ref[:, lanes])
        msg_ref[kinds : kinds + 1, lanes] = total[0:1]
    msg_ref[kinds + 1 :, :] = jnp.zeros((WORDS - kinds - 1, slots), jnp.float32)
    edge_read.wait()
    for side in range(2):
        for k in range(kinds):
            r, at = edge_place(slots, k, side)
            msg_ref[r : r + 1, at : at + LANES] = edge_ref[side, k : k + 1, :]


def stencil_kernel(state_hbm, out_hbm, edge_ref, state, out, sems, out_sems):
    fields, levels, tile_x, tile_y = state.shape
    reads = [
        pltpu.make_async_copy(state_hbm.at[:, z], state.at[:, z], sems.at[z]) for z in range(levels)
    ]
    writes = [
        pltpu.make_async_copy(out.at[:, z], out_hbm.at[:, z], out_sems.at[z]) for z in range(levels)
    ]
    for read in reads:
        read.start()
    reads[0].wait()
    row = iota((tile_x, tile_y), 0)
    lane = iota((tile_x, tile_y), 1)
    wind = 0.5 * time_step * advect_coef
    across = time_step * diffuse_h
    upward = time_step * diffuse_z
    keep = 1.0 - 4.0 * across - 2.0 * upward
    for z in range(levels):
        if z + 1 < levels:
            reads[z + 1].wait()
        u = wind * state[0, z]
        v = wind * state[1, z]
        east_gain = jnp.where(row == tile_x - 1, 0.0, across - u)
        west_gain = jnp.where(row == 0, 0.0, across + u)
        north_gain = jnp.where(lane == tile_y - 1, 0.0, across - v)
        south_gain = jnp.where(lane == 0, 0.0, across + v)
        for f in range(fields):
            cell = state[f, z]
            edge_ref[0, f * levels + z : f * levels + z + 1, :] = cell[0:1]
            edge_ref[1, f * levels + z : f * levels + z + 1, :] = cell[tile_x - 1 :]
            stacked = state[f, min(z + 1, levels - 1)] + state[f, max(z - 1, 0)]
            total = keep * cell + upward * stacked
            total = total + east_gain * pltpu.roll(cell, tile_x - 1, 0)
            total = total + west_gain * pltpu.roll(cell, 1, 0)
            total = total + north_gain * pltpu.roll(cell, tile_y - 1, 1)
            total = total + south_gain * pltpu.roll(cell, 1, 1)
            out[f, z] = total
        writes[z].start()
    for write in writes:
        write.wait()


def nudge_kernel(stages, bounds_ref, *refs):
    me = lax.axis_index("gx")
    even = lax.rem(lax.axis_index("gy"), 2) == 0
    sum_ref, recv_refs, refs = refs[0], refs[1 : 1 + stages], refs[1 + stages :]
    (terms_ref, gram_ref, ys_ref, wt_ref, give_a, give_b, got_a, got_b,
     base_hbm, out_hbm, num_ref, base, out, spread_ref, in_sem, out_sems) = refs
    kinds, tile_x, tile_y = base.shape
    levels = kinds // 3
    slots = ys_ref.shape[1]
    blocks = slots // RB
    read = pltpu.make_async_copy(base_hbm, base, in_sem)
    read.start()
    num_ref[...] = jnp.zeros_like(num_ref)
    total = sum_ref[0 : kinds + 1, :] + recv_refs[-1][0 : kinds + 1, :]
    averaged = total[0:kinds] / total[kinds : kinds + 1]
    spread_ref[0:kinds, :] = terms_ref[...] - dot(gram_ref[...], averaged, NN, HIGHEST)
    spread_ref[kinds : kinds + 1, :] = jnp.ones((1, slots), jnp.float32)

    y_blocks = tile_y // YB
    for j, b in pair_list(bounds_ref, blocks, y_blocks):
        lanes = pl.ds(pl.multiple_of(j * RB, RB), RB)
        start = pl.multiple_of(jnp.minimum(b, y_blocks - 1) * YB, YB)
        named = (iota((YB, RB), 0) + b * YB).astype(jnp.float32) == ys_ref[0:1, lanes]
        spread = spread_ref[0 : kinds + 1, lanes]
        placed = jnp.where(named[None], spread[:, None, :], 0.0)
        b_hi, b_lo = split2(placed.reshape((kinds + 1) * YB, RB))
        both = dot(b_hi, wt_ref[:, lanes], NT)
        part = both[:, 0:tile_x] + both[:, tile_x:] + dot(b_lo, wt_ref[0:tile_x, lanes], NT)
        num_ref[:, pl.ds(start, YB), :] += part.reshape(kinds + 1, YB, tile_x)

    wind = 0.5 * time_step * advect_coef
    across = time_step * diffuse_h
    scale = time_step * nudge_gain / jnp.maximum(num_ref[kinds], 1.0)
    read.wait()
    for k in range(kinds):
        z = k % levels
        turned = num_ref[k] * scale
        v_row = slice(levels + z, levels + z + 1)
        beyond_a, beyond_b = got_a[k : k + 1, :], got_b[k : k + 1, :]
        v_a, v_b = give_a[v_row, :], give_b[v_row, :]
        north = jnp.where(even, beyond_a, beyond_b) * (across - wind * jnp.where(even, v_a, v_b))
        south = jnp.where(even, beyond_b, beyond_a) * (across + wind * jnp.where(even, v_b, v_a))
        cell_row = iota(turned.shape, 0)
        turned = turned + jnp.where(
            cell_row == 0, south, jnp.where(cell_row == tile_y - 1, north, 0.0)
        )
        out[k] = base[k] + jnp.transpose(turned)
        west = jnp.zeros((1, tile_y), jnp.float32)
        east = jnp.zeros((1, tile_y), jnp.float32)
        for s in range(stages):
            r, at = edge_place(slots, k, 1)
            west = west + jnp.where(me ^ (2 ** (s + 1) - 1) == me - 1, recv_refs[s][r : r + 1, at : at + LANES], 0.0)
            r, at = edge_place(slots, k, 0)
            east = east + jnp.where(me ^ (2 ** (s + 1) - 1) == me + 1, recv_refs[s][r : r + 1, at : at + LANES], 0.0)
        r, at = edge_place(slots, z, 0)
        u_first = sum_ref[r : r + 1, at : at + LANES]
        r, at = edge_place(slots, z, 1)
        u_last = sum_ref[r : r + 1, at : at + LANES]
        out[k, 0:1, :] += west * (across + wind * u_first)
        out[k, tile_x - 1 : tile_x, :] += east * (across - wind * u_last)
        pltpu.make_async_copy(out.at[k], out_hbm.at[k], out_sems.at[k]).start()
    for k in range(kinds):
        pltpu.make_async_copy(out.at[k], out_hbm.at[k], out_sems.at[k]).wait()


def call(kernel, name, out_shape, in_specs, out_specs, scratch=(), vmem=8, flops=0, moved=0):
    return pl.pallas_call(
        kernel,
        name=name,
        out_shape=out_shape,
        in_specs=in_specs,
        out_specs=out_specs,
        scratch_shapes=list(scratch),
        compiler_params=pltpu.CompilerParams(vmem_limit_bytes=vmem * MIB),
        cost_estimate=pl.CostEstimate(flops=flops, bytes_accessed=moved, transcendentals=0),
    )


def local(model_state, obs_val, obs_owner, obs_x, obs_y, cressman, vertical):
    count_x = lax.axis_size("gx")
    count_y = lax.axis_size("gy")
    fields, levels, tile_x, tile_y = model_state.shape
    kinds = fields * levels
    records = obs_val.shape[0]
    width = cressman.shape[0]
    cap = max(2, 2 * records // count_y)
    slots = count_x * count_y * cap
    blocks = slots // RB
    f32, bf16, i32 = jnp.float32, jnp.bfloat16, jnp.int32
    shape = jax.ShapeDtypeStruct
    stages = count_x.bit_length() - 1

    msg, gram = call(
        functools.partial(pack_kernel, count_y, cap),
        "pack_records",
        (shape((count_x * count_y, 8, LANES), f32), shape((kinds, kinds), f32)),
        [HBM] * 5,
        (VMEM, VMEM),
        [pltpu.VMEM((1, records), i32)] * 3
        + [
            pltpu.VMEM(obs_val.shape, f32),
            pltpu.VMEM((kinds, vertical.shape[2]), f32),
            pltpu.SemaphoreType.DMA((5,)),
        ],
        vmem=MOST,
        flops=10**7,
        moved=10**6,
    )(
        obs_owner.reshape(1, records),
        obs_x.reshape(1, records),
        obs_y.reshape(1, records),
        obs_val,
        vertical.reshape(kinds, vertical.shape[2]),
    )
    recv = lax.all_to_all(msg, ("gx", "gy"), split_axis=0, concat_axis=0, tiled=True)

    base, edges = call(
        stencil_kernel,
        "stencil",
        (shape(model_state.shape, f32), shape((2, kinds, tile_y), f32)),
        [HBM],
        (HBM, VMEM),
        [
            pltpu.VMEM(model_state.shape, f32),
            pltpu.VMEM(model_state.shape, f32),
            pltpu.SemaphoreType.DMA((levels,)),
            pltpu.SemaphoreType.DMA((levels,)),
        ],
        vmem=MOST,
        moved=10**7,
    )(model_state)

    state3 = model_state.reshape(kinds, tile_x, tile_y)
    partial, wt, ys, terms, bounds, give_a, give_b = call(
        functools.partial(sums_kernel, cap),
        "column_sums",
        (
            shape((WORDS, slots), f32),
            shape((2 * tile_x, slots), bf16),
            shape((8, slots), f32),
            shape((kinds, slots), f32),
            shape((2 * blocks,), i32),
            shape((kinds, tile_x), f32),
            shape((kinds, tile_x), f32),
        ),
        [VMEM, HBM, HBM, HBM],
        (VMEM, VMEM, VMEM, VMEM, SMEM, VMEM, VMEM),
        [
            pltpu.VMEM((blocks, kinds, 8, RB), f32),
            pltpu.VMEM((2, kinds, tile_y), f32),
            pltpu.VMEM((kinds, tile_x, tile_y), f32),
            pltpu.VMEM((width, tile_x), f32),
            pltpu.VMEM((kinds, tile_y, tile_x), bf16),
            pltpu.VMEM((kinds, tile_y, tile_x), bf16),
            pltpu.VMEM((2 * tile_x, width), bf16),
            pltpu.SemaphoreType.DMA((2 * blocks,)),
            pltpu.SemaphoreType.DMA,
        ],
        vmem=SOME,
        flops=4 * 10**9,
        moved=10**7,
    )(recv, edges, state3, cressman)

    got_a = lax.ppermute(give_a, "gy", [(i, i ^ 1) for i in range(count_y)])
    got_b = lax.ppermute(give_b, "gy", [(i, ((i - 1) ^ 1) + 1) for i in range(1, count_y - 1)])

    summed, received = partial, []
    summing = (jnp.arange(WORDS) < kinds + 1)[:, None]
    for s in range(stages):
        mask = 2 ** (s + 1) - 1
        got = lax.ppermute(summed, "gx", [(i, i ^ mask) for i in range(count_x)])
        received.append(got)
        if s < stages - 1:
            summed = jnp.where(summing, summed + got, summed)

    out = call(
        functools.partial(nudge_kernel, stages),
        "nudge",
        shape((kinds, tile_x, tile_y), f32),
        [SMEM] + [VMEM] * (9 + stages) + [HBM],
        ANY,
        [
            pltpu.VMEM((kinds + 1, tile_y, tile_x), f32),
            pltpu.VMEM((kinds, tile_x, tile_y), f32),
            pltpu.VMEM((kinds, tile_x, tile_y), f32),
            pltpu.VMEM((WORDS, slots), f32),
            pltpu.SemaphoreType.DMA,
            pltpu.SemaphoreType.DMA((kinds,)),
        ],
        vmem=SOME,
        flops=4 * 10**9,
        moved=10**7,
    )(
        bounds, summed, *received, terms, gram, ys, wt,
        give_a, give_b, got_a, got_b, base.reshape(kinds, tile_x, tile_y),
    )
    return out.reshape(model_state.shape)


def solution(mesh):
    in_specs = (
        P(None, None, "gx", "gy"),
        P(("gx", "gy"), None),
        P(("gx", "gy"), None),
        P(("gx", "gy")),
        P(("gx", "gy")),
        P(None, "gx"),
        P(),
    )
    out_specs = P(None, None, "gx", "gy")
    return jax.shard_map(local, mesh=mesh, in_specs=in_specs, out_specs=out_specs, check_vma=False)
```

```python
import functools

import jax
import jax.numpy as jnp
from jax import lax
from jax.experimental import pallas as pl
from jax.experimental.pallas import tpu as pltpu
from jax.sharding import PartitionSpec as P

advect_coef = 0.5
diffuse_h = 0.2
diffuse_z = 0.1
time_step = 0.5
nudge_gain = 1.0
spread_gain = 0.125

LANES = 128
WORDS = 32
LANE_STEP = 32
YB = 16
PARTS = 4
RB = 256
MIB = 1024 * 1024
MOST = 58
SOME = 50

HIGHEST = lax.Precision.HIGHEST
NT = (((1,), (1,)), ((), ()))
NN = (((1,), (0,)), ((), ()))
VMEM = pl.BlockSpec(memory_space=pltpu.VMEM)
ANY = pl.BlockSpec(memory_space=pl.ANY)
SMEM = pl.BlockSpec(memory_space=pltpu.SMEM)
HBM = pl.BlockSpec(memory_space=pltpu.HBM)


def dot(a, b, dims=NN, precision=None):
    return lax.dot_general(a, b, dims, precision=precision, preferred_element_type=jnp.float32)


def split2(value):
    high = value.astype(jnp.bfloat16)
    low = (value - high.astype(jnp.float32)).astype(jnp.bfloat16)
    return high, low


def iota(shape, axis):
    return lax.broadcasted_iota(jnp.int32, shape, axis)


def each(count, action):
    lax.fori_loop(0, count, lambda i, carry: (action(i), carry)[1], 0)


def part_copies(source, target, sem, size):
    def copy(i):
        some = pl.ds(pl.multiple_of(i * size, size), size)
        return pltpu.make_async_copy(source.at[some], target.at[some], sem.at[i])

    return copy


def pack_kernel(count_y, cap, *refs):
    sources, (msg_ref, gram_ref), places, sems = refs[:5], refs[5:7], refs[7:12], refs[12]
    copies = [pltpu.make_async_copy(a, b, sems.at[i]) for i, (a, b) in enumerate(zip(sources, places))]
    for copy in copies:
        copy.start()
    for copy in copies:
        copy.wait()
    owner_ref, x_ref, y_ref, obs_ref, vert_ref = places
    records, kinds = x_ref.shape[1], vert_ref.shape[0]
    levels = kinds // 3
    vert = vert_ref[...]
    terms = []
    for v in range(3):
        obs = obs_ref[:, v * LANES : (v + 1) * LANES]
        terms.append(dot(vert[v * levels : (v + 1) * levels], obs, NT, HIGHEST) * spread_gain)
    row = iota((8, records), 0)
    x_row = jnp.broadcast_to(x_ref[...].astype(jnp.float32), (8, records))
    y_row = jnp.broadcast_to(y_ref[...].astype(jnp.float32) - float(LANES), (8, records))
    head = jnp.where(row == 0, x_row, jnp.where(row == 1, y_row, 0.0))
    payload = jnp.concatenate([head] + terms, axis=0)

    owner = owner_ref[...].astype(jnp.float32)
    owner_lanes = jnp.broadcast_to(owner, (records, records))
    owner_rows = jnp.transpose(owner_lanes)
    earlier = iota((records, records), 0) < iota((records, records), 1)
    same = jnp.where((owner_lanes == owner_rows) & earlier, 1.0, 0.0)
    rank = jnp.sum(same, axis=0, keepdims=True)
    slot = owner * float(cap) + rank
    places = count_y * cap
    pick = jnp.where(iota((places, records), 0).astype(jnp.float32) == slot, 1.0, 0.0)
    out = dot(payload, pick, NT, HIGHEST)

    lane = iota((8, LANES), 1)
    for c in range(count_y):
        chunk = (c * cap) // LANES
        offset = (c * cap) % LANES
        block = jnp.zeros((8, LANES), jnp.float32)
        for j in range(WORDS // 8):
            part = out[8 * j : 8 * j + 8, chunk * LANES : (chunk + 1) * LANES]
            shift = (LANE_STEP * j - offset) % LANES
            if shift:
                part = pltpu.roll(part, shift, 1)
            inside = (lane >= LANE_STEP * j) & (lane < LANE_STEP * j + cap)
            block = jnp.where(inside, part, block)
        for g in range(msg_ref.shape[0] // count_y):
            msg_ref[g * count_y + c] = block

    gram = dot(vert, vert, NT, HIGHEST) * spread_gain
    alike = (iota((kinds, kinds), 0) // levels) == (iota((kinds, kinds), 1) // levels)
    gram_ref[...] = jnp.where(alike, gram, 0.0)


def unpack(recv_ref, cap, j):
    devices = recv_ref.shape[0]
    per = LANES // cap
    lane = iota((8, LANES), 1)
    chunks = []
    for q in range(devices // per):
        block = jnp.zeros((8, LANES), jnp.float32)
        for t in range(per):
            part = recv_ref[q * per + t]
            shift = (cap * t - LANE_STEP * j) % LANES
            if shift:
                part = pltpu.roll(part, shift, 1)
            inside = (lane >= cap * t) & (lane < cap * t + cap)
            block = jnp.where(inside, part, block)
        chunks.append(block)
    return chunks


def pair_list(bounds_ref, blocks, y_blocks):
    j, b = jnp.int32(0), bounds_ref[0]
    pairs = []
    for _ in range(blocks + y_blocks - 1):
        valid = (j < blocks) & (b < bounds_ref[2 * jnp.minimum(j, blocks - 1) + 1])
        pairs.append((jnp.minimum(j, blocks - 1), jnp.where(valid, b, y_blocks + 1)))
        more = b + 1 < bounds_ref[2 * jnp.minimum(j, blocks - 1) + 1]
        following = jnp.minimum(j + 1, blocks - 1)
        b = jnp.where(more, b + 1, bounds_ref[2 * following])
        j = jnp.where(more, j, jnp.minimum(j + 1, blocks))
    return pairs


def edge_place(slots, k, side):
    per = slots // LANES
    rows = -(-24 // per)
    return pl.ds(25 + side * rows + k // per, 1), pl.ds((k % per) * LANES, LANES)


def sums_kernel(
    cap, recv_ref, base_hbm, state_hbm, cress_hbm,
    msg_ref, wt_ref, ys_ref, terms_ref, bounds_ref, give_a_ref, give_b_ref,
    acc_ref, state, cress, mt_hi, mt_lo, ct, cress_sems, state_sems,
):
    kinds, tile_x, tile_y = state.shape
    width = cress.shape[0]
    blocks = recv_ref.shape[0] * cap // RB
    cress_read = part_copies(cress_hbm, cress, cress_sems, width // PARTS)
    state_read = part_copies(state_hbm, state, state_sems, kinds // PARTS)
    each(PARTS, lambda i: cress_read(i).start())
    each(PARTS, lambda i: state_read(i).start())
    slots = recv_ref.shape[0] * cap
    chunks = slots // LANES

    groups = [unpack(recv_ref, cap, j) for j in range(WORDS // 8)]
    keys = []
    for c in range(chunks):
        place = (iota((1, LANES), 1) + c * LANES).astype(jnp.float32)
        keys.append((groups[0][c][1:2] + float(tile_y)) * float(slots) + place)
    counts = [jnp.zeros((8, LANES), jnp.float32) for _ in range(chunks)]
    for c in range(chunks):
        column = jnp.transpose(jnp.broadcast_to(keys[c], (LANES, LANES)))
        for d in range(chunks):
            less = jnp.where(column < keys[d], 1.0, 0.0)
            counts[d] = counts[d] + jnp.sum(less.reshape(LANES // 8, 8, LANES), axis=0)
    rank = jnp.concatenate([jnp.sum(count, axis=0, keepdims=True) for count in counts], axis=1)

    rows = []
    head = jnp.concatenate(groups[0], axis=1)
    x_high = jnp.floor(head[0:1] * 0.0625)
    row = iota((8, slots), 0)
    top = jnp.where(
        row == 0,
        jnp.broadcast_to(x_high, (8, slots)),
        jnp.where(
            row == 1,
            jnp.broadcast_to(head[0:1] - 16.0 * x_high, (8, slots)),
            jnp.where(row == 2, jnp.broadcast_to(head[1:2] + float(tile_y), (8, slots)), 0.0),
        ),
    )
    words = jnp.concatenate([jnp.concatenate(group, axis=1) for group in groups[1:]], axis=0)
    high = words.astype(jnp.bfloat16).astype(jnp.float32)
    middle = (words - high).astype(jnp.bfloat16).astype(jnp.float32)
    low = words - high - middle
    table = jnp.concatenate([top, high, middle, low], axis=0).astype(jnp.bfloat16)

    even = lax.rem(lax.axis_index("gy"), 2) == 0
    x_rows = []
    for j in range(blocks):
        lanes = slice(j * RB, (j + 1) * RB)
        place = (iota((RB, slots), 0) + j * RB).astype(jnp.float32)
        pick = jnp.where(place == rank, 1.0, 0.0).astype(jnp.bfloat16)
        ordered = dot(table, pick, NT)
        x_rows.append(ordered[0:1] * 16.0 + ordered[1:2])
        ys = ordered[2:3]
        ys_ref[:, lanes] = jnp.broadcast_to(ys, (8, RB))
        terms_ref[:, lanes] = ordered[8:32] + ordered[32:56] + ordered[56:80]
        least = jnp.min(ys).astype(jnp.int32)
        most = jnp.minimum(jnp.max(ys).astype(jnp.int32), tile_y - 1)
        bounds_ref[2 * j] = least // YB
        bounds_ref[2 * j + 1] = most // YB + 1

    each(PARTS, lambda i: cress_read(i).wait())
    for i in range(width // LANES):
        rows = slice(i * LANES, (i + 1) * LANES)
        high, low = split2(jnp.transpose(cress[rows, :]))
        ct[0:tile_x, rows] = high
        ct[tile_x:, rows] = low

    def gather(j):
        hot = jnp.where(iota((width, RB), 0).astype(jnp.float32) == x_rows[j], 1.0, 0.0)
        wt = dot(ct[...], hot.astype(jnp.bfloat16))
        wt_ref[:, j * RB : (j + 1) * RB] = wt.astype(jnp.bfloat16)

    half = blocks // 2
    for j in range(half):
        gather(j)
    each(PARTS, lambda i: state_read(i).wait())
    planes = kinds // (blocks - half)
    for j in range(half, blocks):
        gather(j)
        for k in range((j - half) * planes, (j - half + 1) * planes):
            turned = jnp.transpose(state[k])
            high, low = split2(turned)
            mt_hi[k] = high
            mt_lo[k] = low
            first, last = turned[0:1], turned[tile_y - 1 :]
            give_a_ref[k : k + 1, :] = jnp.where(even, last, first)
            give_b_ref[k : k + 1, :] = jnp.where(even, first, last)

    acc_ref[...] = jnp.zeros_like(acc_ref)
    y_blocks = tile_y // YB
    for j, b in pair_list(bounds_ref, blocks, y_blocks):
        lanes = pl.ds(pl.multiple_of(j * RB, RB), RB)
        start = pl.multiple_of(jnp.minimum(b, y_blocks - 1) * YB, YB)
        a_hi = mt_hi[:, pl.ds(start, YB), :].reshape(kinds * YB, tile_x)
        a_lo = mt_lo[:, pl.ds(start, YB), :].reshape(kinds * YB, tile_x)
        w_hi = wt_ref[0:tile_x, lanes]
        part = dot(jnp.concatenate([a_hi, a_hi], axis=1), wt_ref[:, lanes]) + dot(a_lo, w_hi)
        named = (iota((YB, RB), 0) + b * YB).astype(jnp.float32) == ys_ref[0:1, lanes]
        kept = jnp.where(named[None], part.reshape(kinds, YB, RB), 0.0)
        acc_ref[j] += kept[:, :8] + kept[:, 8:]

    ones = jnp.ones((8, 2 * tile_x), jnp.bfloat16)
    for j in range(blocks):
        lanes = slice(j * RB, (j + 1) * RB)
        msg_ref[0:kinds, lanes] = jnp.sum(acc_ref[j], axis=1)
        total = dot(ones, wt_ref[:, lanes])
        msg_ref[kinds : kinds + 1, lanes] = total[0:1]
    msg_ref[kinds + 1 :, :] = jnp.zeros((WORDS - kinds - 1, slots), jnp.float32)
    for side, edge in enumerate((0, tile_x - 1)):
        for k in range(kinds):
            msg_ref[edge_place(slots, k, side)] = state[k, edge : edge + 1, :]


def stencil_kernel(state_hbm, out_hbm, state, out, in_sems, out_sems):
    fields, levels, tile_x, tile_y = state.shape

    def read(z):
        return pltpu.make_async_copy(state_hbm.at[:, z], state.at[:, z], in_sems.at[z])

    def write(z):
        return pltpu.make_async_copy(out.at[:, z], out_hbm.at[:, z], out_sems.at[z])

    each(levels, lambda z: read(z).start())
    read(0).wait()
    row = iota((tile_x, tile_y), 0)
    lane = iota((tile_x, tile_y), 1)
    wind = 0.5 * time_step * advect_coef
    across = time_step * diffuse_h
    upward = time_step * diffuse_z
    keep = 1.0 - 4.0 * across - 2.0 * upward

    def level(z):
        @pl.when(z + 1 < levels)
        def _():
            read(z + 1).wait()

        u = wind * state[0, z]
        v = wind * state[1, z]
        east_gain = jnp.where(row == tile_x - 1, 0.0, across - u)
        west_gain = jnp.where(row == 0, 0.0, across + u)
        north_gain = jnp.where(lane == tile_y - 1, 0.0, across - v)
        south_gain = jnp.where(lane == 0, 0.0, across + v)
        for f in range(fields):
            cell = state[f, z]
            stacked = state[f, jnp.minimum(z + 1, levels - 1)] + state[f, jnp.maximum(z - 1, 0)]
            total = keep * cell + upward * stacked
            total = total + east_gain * pltpu.roll(cell, tile_x - 1, 0)
            total = total + west_gain * pltpu.roll(cell, 1, 0)
            total = total + north_gain * pltpu.roll(cell, tile_y - 1, 1)
            total = total + south_gain * pltpu.roll(cell, 1, 1)
            out[f, z] = total
        write(z).start()

    each(levels, level)
    each(levels, lambda z: write(z).wait())


def nudge_kernel(stages, bounds_ref, *refs):
    me = lax.axis_index("gx")
    even = lax.rem(lax.axis_index("gy"), 2) == 0
    sum_ref, recv_refs, refs = refs[0], refs[1 : 1 + stages], refs[1 + stages :]
    (terms_ref, gram_ref, ys_ref, wt_ref, give_a, give_b, got_a, got_b,
     base_hbm, out_hbm, num_ref, base, out, spread_ref, y_add, x_add, in_sems, out_sems) = refs
    kinds, tile_x, tile_y = base.shape
    levels = kinds // 3
    slots = ys_ref.shape[1]
    blocks = slots // RB
    read = part_copies(base_hbm, base, in_sems, kinds // PARTS)
    each(PARTS, lambda i: read(i).start())
    num_ref[...] = jnp.zeros_like(num_ref)
    total = sum_ref[0 : kinds + 1, :] + recv_refs[-1][0 : kinds + 1, :]
    averaged = total[0:kinds] / total[kinds : kinds + 1]
    spread_ref[0:kinds, :] = terms_ref[...] - dot(gram_ref[...], averaged, NN, HIGHEST)
    spread_ref[kinds : kinds + 1, :] = jnp.ones((1, slots), jnp.float32)

    y_blocks = tile_y // YB
    for j, b in pair_list(bounds_ref, blocks, y_blocks):
        lanes = pl.ds(pl.multiple_of(j * RB, RB), RB)
        start = pl.multiple_of(jnp.minimum(b, y_blocks - 1) * YB, YB)
        named = (iota((YB, RB), 0) + b * YB).astype(jnp.float32) == ys_ref[0:1, lanes]
        spread = spread_ref[0 : kinds + 1, lanes]
        placed = jnp.where(named[None], spread[:, None, :], 0.0)
        b_hi, b_lo = split2(placed.reshape((kinds + 1) * YB, RB))
        both = dot(b_hi, wt_ref[:, lanes], NT)
        part = both[:, 0:tile_x] + both[:, tile_x:] + dot(b_lo, wt_ref[0:tile_x, lanes], NT)
        num_ref[:, pl.ds(start, YB), :] += part.reshape(kinds + 1, YB, tile_x)

    wind = 0.5 * time_step * advect_coef
    across = time_step * diffuse_h
    scale = time_step * nudge_gain / jnp.maximum(num_ref[kinds], 1.0)
    v_rows = slice(levels, 2 * levels)
    v_a = jnp.concatenate([give_a[v_rows, :]] * 3, axis=0)
    v_b = jnp.concatenate([give_b[v_rows, :]] * 3, axis=0)
    north = jnp.where(even, got_a[...], got_b[...]) * (across - wind * jnp.where(even, v_a, v_b))
    south = jnp.where(even, got_b[...], got_a[...]) * (across + wind * jnp.where(even, v_b, v_a))
    for k in range(kinds):
        y_add[k, 0:1, :] = south[k : k + 1, :]
        y_add[k, 1:2, :] = north[k : k + 1, :]
        west = jnp.zeros((1, tile_y), jnp.float32)
        east = jnp.zeros((1, tile_y), jnp.float32)
        for s in range(stages):
            partner = me ^ (2 ** (s + 1) - 1)
            west = west + jnp.where(partner == me - 1, recv_refs[s][edge_place(slots, k, 1)], 0.0)
            east = east + jnp.where(partner == me + 1, recv_refs[s][edge_place(slots, k, 0)], 0.0)
        z = k % levels
        x_add[k, 0:1, :] = west * (across + wind * sum_ref[edge_place(slots, z, 0)])
        x_add[k, 1:2, :] = east * (across - wind * sum_ref[edge_place(slots, z, 1)])
    each(PARTS, lambda i: read(i).wait())
    cell_row = iota((tile_y, tile_x), 0)

    def finish(k):
        edges = jnp.where(
            cell_row == 0, y_add[k, 0:1, :], jnp.where(cell_row == tile_y - 1, y_add[k, 1:2, :], 0.0)
        )
        out[k] = base[k] + jnp.transpose(num_ref[k] * scale + edges)
        out[k, 0:1, :] += x_add[k, 0:1, :]
        out[k, tile_x - 1 : tile_x, :] += x_add[k, 1:2, :]
        pltpu.make_async_copy(out.at[k], out_hbm.at[k], out_sems.at[k]).start()

    def finish_some(i):
        for n in range(levels):
            finish(i * levels + n)

    each(kinds // levels, finish_some)
    each(kinds, lambda k: pltpu.make_async_copy(out.at[k], out_hbm.at[k], out_sems.at[k]).wait())


def call(kernel, name, out_shape, in_specs, out_specs, scratch=(), vmem=8, flops=0, moved=0):
    return pl.pallas_call(
        kernel,
        name=name,
        out_shape=out_shape,
        in_specs=in_specs,
        out_specs=out_specs,
        scratch_shapes=list(scratch),
        compiler_params=pltpu.CompilerParams(vmem_limit_bytes=vmem * MIB),
        cost_estimate=pl.CostEstimate(flops=flops, bytes_accessed=moved, transcendentals=0),
    )


def local(model_state, obs_val, obs_owner, obs_x, obs_y, cressman, vertical):
    count_x = lax.axis_size("gx")
    count_y = lax.axis_size("gy")
    fields, levels, tile_x, tile_y = model_state.shape
    kinds = fields * levels
    records = obs_val.shape[0]
    width = cressman.shape[0]
    cap = max(2, 2 * records // count_y)
    slots = count_x * count_y * cap
    blocks = slots // RB
    f32, bf16, i32 = jnp.float32, jnp.bfloat16, jnp.int32
    shape = jax.ShapeDtypeStruct
    stages = count_x.bit_length() - 1

    msg, gram = call(
        functools.partial(pack_kernel, count_y, cap),
        "pack_records",
        (shape((count_x * count_y, 8, LANES), f32), shape((kinds, kinds), f32)),
        [HBM] * 5,
        (VMEM, VMEM),
        [pltpu.VMEM((1, records), i32)] * 3
        + [
            pltpu.VMEM(obs_val.shape, f32),
            pltpu.VMEM((kinds, vertical.shape[2]), f32),
            pltpu.SemaphoreType.DMA((5,)),
        ],
        vmem=MOST,
        flops=10**7,
        moved=10**6,
    )(
        obs_owner.reshape(1, records),
        obs_x.reshape(1, records),
        obs_y.reshape(1, records),
        obs_val,
        vertical.reshape(kinds, vertical.shape[2]),
    )
    recv = lax.all_to_all(msg, ("gx", "gy"), split_axis=0, concat_axis=0, tiled=True)

    base = call(
        stencil_kernel,
        "stencil",
        shape(model_state.shape, f32),
        [HBM],
        HBM,
        [
            pltpu.VMEM(model_state.shape, f32),
            pltpu.VMEM(model_state.shape, f32),
            pltpu.SemaphoreType.DMA((levels,)),
            pltpu.SemaphoreType.DMA((levels,)),
        ],
        vmem=MOST,
        moved=10**7,
    )(model_state)

    state3 = model_state.reshape(kinds, tile_x, tile_y)
    partial, wt, ys, terms, bounds, give_a, give_b = call(
        functools.partial(sums_kernel, cap),
        "column_sums",
        (
            shape((WORDS, slots), f32),
            shape((2 * tile_x, slots), bf16),
            shape((8, slots), f32),
            shape((kinds, slots), f32),
            shape((2 * blocks,), i32),
            shape((kinds, tile_x), f32),
            shape((kinds, tile_x), f32),
        ),
        [VMEM, HBM, HBM, HBM],
        (VMEM, VMEM, VMEM, VMEM, SMEM, VMEM, VMEM),
        [
            pltpu.VMEM((blocks, kinds, 8, RB), f32),
            pltpu.VMEM((kinds, tile_x, tile_y), f32),
            pltpu.VMEM((width, tile_x), f32),
            pltpu.VMEM((kinds, tile_y, tile_x), bf16),
            pltpu.VMEM((kinds, tile_y, tile_x), bf16),
            pltpu.VMEM((2 * tile_x, width), bf16),
            pltpu.SemaphoreType.DMA((PARTS,)),
            pltpu.SemaphoreType.DMA((PARTS,)),
        ],
        vmem=SOME,
        flops=4 * 10**9,
        moved=10**7,
    )(recv, base, state3, cressman)

    got_a = lax.ppermute(give_a, "gy", [(i, i ^ 1) for i in range(count_y)])
    got_b = lax.ppermute(give_b, "gy", [(i, ((i - 1) ^ 1) + 1) for i in range(1, count_y - 1)])

    summed, received = partial, []
    summing = (jnp.arange(WORDS) < kinds + 1)[:, None]
    for s in range(stages):
        mask = 2 ** (s + 1) - 1
        got = lax.ppermute(summed, "gx", [(i, i ^ mask) for i in range(count_x)])
        received.append(got)
        if s < stages - 1:
            summed = jnp.where(summing, summed + got, summed)

    out = call(
        functools.partial(nudge_kernel, stages),
        "nudge",
        shape((kinds, tile_x, tile_y), f32),
        [SMEM] + [VMEM] * (9 + stages) + [HBM],
        ANY,
        [
            pltpu.VMEM((kinds + 1, tile_y, tile_x), f32),
            pltpu.VMEM((kinds, tile_x, tile_y), f32),
            pltpu.VMEM((kinds, tile_x, tile_y), f32),
            pltpu.VMEM((WORDS, slots), f32),
            pltpu.VMEM((kinds, 2, tile_x), f32),
            pltpu.VMEM((kinds, 2, tile_y), f32),
            pltpu.SemaphoreType.DMA((PARTS,)),
            pltpu.SemaphoreType.DMA((kinds,)),
        ],
        vmem=SOME,
        flops=4 * 10**9,
        moved=10**7,
    )(
        bounds, summed, *received, terms, gram, ys, wt,
        give_a, give_b, got_a, got_b, base.reshape(kinds, tile_x, tile_y),
    )
    return out.reshape(model_state.shape)


def solution(mesh):
    in_specs = (
        P(None, None, "gx", "gy"),
        P(("gx", "gy"), None),
        P(("gx", "gy"), None),
        P(("gx", "gy")),
        P(("gx", "gy")),
        P(None, "gx"),
        P(),
    )
    out_specs = P(None, None, "gx", "gy")
    return jax.shard_map(local, mesh=mesh, in_specs=in_specs, out_specs=out_specs, check_vma=False)
```

```python
import functools

import jax
import jax.numpy as jnp
from jax import lax
from jax.experimental import pallas as pl
from jax.experimental.pallas import tpu as pltpu
from jax.sharding import PartitionSpec as P

advect_coef = 0.5
diffuse_h = 0.2
diffuse_z = 0.1
time_step = 0.5
nudge_gain = 1.0
spread_gain = 0.125

LANES = 128
WORDS = 32
LANE_STEP = 32
YB = 16
PARTS = 4
RB = 256
MIB = 1024 * 1024
MOST = 58
SOME = 50

HIGHEST = lax.Precision.HIGHEST
NT = (((1,), (1,)), ((), ()))
NN = (((1,), (0,)), ((), ()))
VMEM = pl.BlockSpec(memory_space=pltpu.VMEM)
ANY = pl.BlockSpec(memory_space=pl.ANY)
SMEM = pl.BlockSpec(memory_space=pltpu.SMEM)
HBM = pl.BlockSpec(memory_space=pltpu.HBM)


def dot(a, b, dims=NN, precision=None):
    return lax.dot_general(a, b, dims, precision=precision, preferred_element_type=jnp.float32)


def split2(value):
    high = value.astype(jnp.bfloat16)
    low = (value - high.astype(jnp.float32)).astype(jnp.bfloat16)
    return high, low


def dot3(a, b, dims=NN):
    (a_hi, a_lo), (b_hi, b_lo) = [[half.astype(jnp.float32) for half in split2(m)] for m in (a, b)]
    a3 = jnp.concatenate([a_hi, a_hi, a_lo], axis=dims[0][0][0]).astype(jnp.bfloat16)
    b3 = jnp.concatenate([b_hi, b_lo, b_hi], axis=dims[0][1][0]).astype(jnp.bfloat16)
    return dot(a3, b3, dims)


def iota(shape, axis):
    return lax.broadcasted_iota(jnp.int32, shape, axis)


def each(count, action):
    lax.fori_loop(0, count, lambda i, carry: (action(i), carry)[1], 0)


def part_copies(source, target, sem, size):
    def copy(i):
        some = pl.ds(pl.multiple_of(i * size, size), size)
        return pltpu.make_async_copy(source.at[some], target.at[some], sem.at[i])

    return copy


def pack_kernel(count_y, cap, *refs):
    sources, (msg_ref, gram_ref), places, sems = refs[:5], refs[5:7], refs[7:12], refs[12]
    copies = [pltpu.make_async_copy(a, b, sems.at[i]) for i, (a, b) in enumerate(zip(sources, places))]
    for copy in copies:
        copy.start()
    for copy in copies:
        copy.wait()
    owner_ref, x_ref, y_ref, obs_ref, vert_ref = places
    records, kinds = x_ref.shape[1], vert_ref.shape[0]
    levels = kinds // 3
    vert = vert_ref[...]
    terms = []
    for v in range(3):
        obs = obs_ref[:, v * LANES : (v + 1) * LANES]
        terms.append(dot3(vert[v * levels : (v + 1) * levels], obs, NT) * spread_gain)
    row = iota((8, records), 0)
    x_row = jnp.broadcast_to(x_ref[...].astype(jnp.float32), (8, records))
    y_row = jnp.broadcast_to(y_ref[...].astype(jnp.float32) - float(LANES), (8, records))
    head = jnp.where(row == 0, x_row, jnp.where(row == 1, y_row, 0.0))
    payload = jnp.concatenate([head] + terms, axis=0)

    owner = owner_ref[...].astype(jnp.float32)
    owner_lanes = jnp.broadcast_to(owner, (records, records))
    owner_rows = jnp.transpose(owner_lanes)
    earlier = iota((records, records), 0) < iota((records, records), 1)
    same = jnp.where((owner_lanes == owner_rows) & earlier, 1.0, 0.0)
    rank = jnp.sum(same, axis=0, keepdims=True)
    slot = owner * float(cap) + rank
    places = count_y * cap
    pick = jnp.where(iota((places, records), 0).astype(jnp.float32) == slot, 1.0, 0.0)
    high = payload.astype(jnp.bfloat16).astype(jnp.float32)
    middle = (payload - high).astype(jnp.bfloat16).astype(jnp.float32)
    parts = jnp.concatenate([high, middle, payload - high - middle], axis=0).astype(jnp.bfloat16)
    out = dot(parts, pick.astype(jnp.bfloat16), NT)
    out = out[0:WORDS] + out[WORDS : 2 * WORDS] + out[2 * WORDS :]

    lane = iota((8, LANES), 1)
    for c in range(count_y):
        chunk = (c * cap) // LANES
        offset = (c * cap) % LANES
        block = jnp.zeros((8, LANES), jnp.float32)
        for j in range(WORDS // 8):
            part = out[8 * j : 8 * j + 8, chunk * LANES : (chunk + 1) * LANES]
            shift = (LANE_STEP * j - offset) % LANES
            if shift:
                part = pltpu.roll(part, shift, 1)
            inside = (lane >= LANE_STEP * j) & (lane < LANE_STEP * j + cap)
            block = jnp.where(inside, part, block)
        for g in range(msg_ref.shape[0] // count_y):
            msg_ref[g * count_y + c] = block

    gram = dot(vert, vert, NT, HIGHEST) * spread_gain
    alike = (iota((kinds, kinds), 0) // levels) == (iota((kinds, kinds), 1) // levels)
    gram_ref[...] = jnp.where(alike, gram, 0.0)


def unpack(recv_ref, cap, j):
    devices = recv_ref.shape[0]
    per = LANES // cap
    lane = iota((8, LANES), 1)
    chunks = []
    for q in range(devices // per):
        block = jnp.zeros((8, LANES), jnp.float32)
        for t in range(per):
            part = recv_ref[q * per + t]
            shift = (cap * t - LANE_STEP * j) % LANES
            if shift:
                part = pltpu.roll(part, shift, 1)
            inside = (lane >= cap * t) & (lane < cap * t + cap)
            block = jnp.where(inside, part, block)
        chunks.append(block)
    return chunks


def pair_list(bounds_ref, blocks, y_blocks):
    j, b = jnp.int32(0), bounds_ref[0]
    pairs = []
    for _ in range(blocks + y_blocks - 1):
        valid = (j < blocks) & (b < bounds_ref[2 * jnp.minimum(j, blocks - 1) + 1])
        pairs.append((jnp.minimum(j, blocks - 1), jnp.where(valid, b, y_blocks + 1)))
        more = b + 1 < bounds_ref[2 * jnp.minimum(j, blocks - 1) + 1]
        following = jnp.minimum(j + 1, blocks - 1)
        b = jnp.where(more, b + 1, bounds_ref[2 * following])
        j = jnp.where(more, j, jnp.minimum(j + 1, blocks))
    return pairs


def edge_place(slots, k, side):
    per = slots // LANES
    rows = -(-24 // per)
    return pl.ds(25 + side * rows + k // per, 1), pl.ds((k % per) * LANES, LANES)


def sums_kernel(
    cap, recv_ref, base_hbm, state_hbm, cress_hbm,
    msg_ref, wt_ref, ys_ref, terms_ref, bounds_ref, give_a_ref, give_b_ref,
    state, cress, mt_hi, mt_lo, ct, cress_sems, state_sems,
):
    kinds, tile_x, tile_y = state.shape
    width = cress.shape[0]
    blocks = recv_ref.shape[0] * cap // RB
    cress_read = part_copies(cress_hbm, cress, cress_sems, width // PARTS)
    state_read = part_copies(state_hbm, state, state_sems, kinds // PARTS)
    each(PARTS, lambda i: cress_read(i).start())
    each(PARTS, lambda i: state_read(i).start())
    slots = recv_ref.shape[0] * cap
    chunks = slots // LANES

    groups = [unpack(recv_ref, cap, j) for j in range(WORDS // 8)]
    keys = []
    for c in range(chunks):
        place = (iota((1, LANES), 1) + c * LANES).astype(jnp.float32)
        keys.append((groups[0][c][1:2] + float(tile_y)) * float(slots) + place)
    counts = [jnp.zeros((8, LANES), jnp.float32) for _ in range(chunks)]
    for c in range(chunks):
        column = jnp.transpose(jnp.broadcast_to(keys[c], (LANES, LANES)))
        for d in range(chunks):
            less = jnp.where(column < keys[d], 1.0, 0.0)
            counts[d] = counts[d] + jnp.sum(less.reshape(LANES // 8, 8, LANES), axis=0)
    rank = jnp.concatenate([jnp.sum(count, axis=0, keepdims=True) for count in counts], axis=1)

    rows = []
    head = jnp.concatenate(groups[0], axis=1)
    x_high = jnp.floor(head[0:1] * 0.0625)
    row = iota((8, slots), 0)
    top = jnp.where(
        row == 0,
        jnp.broadcast_to(x_high, (8, slots)),
        jnp.where(
            row == 1,
            jnp.broadcast_to(head[0:1] - 16.0 * x_high, (8, slots)),
            jnp.where(row == 2, jnp.broadcast_to(head[1:2] + float(tile_y), (8, slots)), 0.0),
        ),
    )
    words = jnp.concatenate([jnp.concatenate(group, axis=1) for group in groups[1:]], axis=0)
    high = words.astype(jnp.bfloat16).astype(jnp.float32)
    middle = (words - high).astype(jnp.bfloat16).astype(jnp.float32)
    low = words - high - middle
    table = jnp.concatenate([top, high, middle, low], axis=0).astype(jnp.bfloat16)

    even = lax.rem(lax.axis_index("gy"), 2) == 0
    x_rows = []
    for j in range(blocks):
        lanes = slice(j * RB, (j + 1) * RB)
        place = (iota((RB, slots), 0) + j * RB).astype(jnp.float32)
        pick = jnp.where(place == rank, 1.0, 0.0).astype(jnp.bfloat16)
        ordered = dot(table, pick, NT)
        x_rows.append(ordered[0:1] * 16.0 + ordered[1:2])
        ys = ordered[2:3]
        ys_ref[:, lanes] = jnp.broadcast_to(ys, (8, RB))
        terms_ref[:, lanes] = ordered[8:32] + ordered[32:56] + ordered[56:80]
        least = jnp.min(ys).astype(jnp.int32)
        most = jnp.minimum(jnp.max(ys).astype(jnp.int32), tile_y - 1)
        bounds_ref[2 * j] = least // YB
        bounds_ref[2 * j + 1] = most // YB + 1

    each(PARTS, lambda i: cress_read(i).wait())
    for i in range(width // LANES):
        rows = slice(i * LANES, (i + 1) * LANES)
        high, low = split2(jnp.transpose(cress[rows, :]))
        ct[0:tile_x, rows] = high
        ct[tile_x:, rows] = low

    def gather(j):
        hot = jnp.where(iota((width, RB), 0).astype(jnp.float32) == x_rows[j], 1.0, 0.0)
        wt = dot(ct[...], hot.astype(jnp.bfloat16))
        wt_ref[:, j * RB : (j + 1) * RB] = wt.astype(jnp.bfloat16)

    half = blocks // 2
    for j in range(half):
        gather(j)
    each(PARTS, lambda i: state_read(i).wait())
    planes = kinds // (blocks - half)
    for j in range(half, blocks):
        gather(j)
        for k in range((j - half) * planes, (j - half + 1) * planes):
            turned = jnp.transpose(state[k])
            high, low = split2(turned)
            mt_hi[k] = high
            mt_lo[k] = low
            first, last = turned[0:1], turned[tile_y - 1 :]
            give_a_ref[k : k + 1, :] = jnp.where(even, last, first)
            give_b_ref[k : k + 1, :] = jnp.where(even, first, last)

    before = running = None
    y_blocks = tile_y // YB
    for j, b in pair_list(bounds_ref, blocks, y_blocks):
        lanes = pl.ds(pl.multiple_of(j * RB, RB), RB)
        start = pl.multiple_of(jnp.minimum(b, y_blocks - 1) * YB, YB)
        a_hi = mt_hi[:, pl.ds(start, YB), :].reshape(kinds * YB, tile_x)
        a_lo = mt_lo[:, pl.ds(start, YB), :].reshape(kinds * YB, tile_x)
        w_hi = wt_ref[0:tile_x, lanes]
        part = dot(jnp.concatenate([a_hi, a_hi], axis=1), wt_ref[:, lanes]) + dot(a_lo, w_hi)
        named = (iota((YB, RB), 0) + b * YB).astype(jnp.float32) == ys_ref[0:1, lanes]
        kept = jnp.where(named[None], part.reshape(kinds, YB, RB), 0.0)
        summed = jnp.sum(kept[:, :8] + kept[:, 8:], axis=1)
        running = summed if before is None else summed + jnp.where(j == before, running, 0.0)
        before = j
        msg_ref[0:kinds, lanes] = running

    ones = jnp.ones((8, 2 * tile_x), jnp.bfloat16)
    for j in range(blocks):
        lanes = slice(j * RB, (j + 1) * RB)
        total = dot(ones, wt_ref[:, lanes])
        msg_ref[kinds : kinds + 1, lanes] = total[0:1]
    msg_ref[kinds + 1 :, :] = jnp.zeros((WORDS - kinds - 1, slots), jnp.float32)
    for side, edge in enumerate((0, tile_x - 1)):
        for k in range(kinds):
            msg_ref[edge_place(slots, k, side)] = state[k, edge : edge + 1, :]


def stencil_kernel(state_hbm, out_hbm, state, out, in_sems, out_sems):
    fields, levels, tile_x, tile_y = state.shape

    def read(z):
        return pltpu.make_async_copy(state_hbm.at[:, z], state.at[:, z], in_sems.at[z])

    def write(z):
        return pltpu.make_async_copy(out.at[:, z], out_hbm.at[:, z], out_sems.at[z])

    each(levels, lambda z: read(z).start())
    read(0).wait()
    row = iota((tile_x, tile_y), 0)
    lane = iota((tile_x, tile_y), 1)
    wind = 0.5 * time_step * advect_coef
    across = time_step * diffuse_h
    upward = time_step * diffuse_z
    keep = 1.0 - 4.0 * across - 2.0 * upward

    def level(z):
        @pl.when(z + 1 < levels)
        def _():
            read(z + 1).wait()

        u = wind * state[0, z]
        v = wind * state[1, z]
        east_gain = jnp.where(row == tile_x - 1, 0.0, across - u)
        west_gain = jnp.where(row == 0, 0.0, across + u)
        north_gain = jnp.where(lane == tile_y - 1, 0.0, across - v)
        south_gain = jnp.where(lane == 0, 0.0, across + v)
        for f in range(fields):
            cell = state[f, z]
            stacked = state[f, jnp.minimum(z + 1, levels - 1)] + state[f, jnp.maximum(z - 1, 0)]
            total = keep * cell + upward * stacked
            total = total + east_gain * pltpu.roll(cell, tile_x - 1, 0)
            total = total + west_gain * pltpu.roll(cell, 1, 0)
            total = total + north_gain * pltpu.roll(cell, tile_y - 1, 1)
            total = total + south_gain * pltpu.roll(cell, 1, 1)
            out[f, z] = total
        write(z).start()

    each(levels, level)
    each(levels, lambda z: write(z).wait())


def nudge_kernel(stages, bounds_ref, *refs):
    me = lax.axis_index("gx")
    even = lax.rem(lax.axis_index("gy"), 2) == 0
    sum_ref, recv_refs, refs = refs[0], refs[1 : 1 + stages], refs[1 + stages :]
    (terms_ref, gram_ref, ys_ref, wt_ref, give_a, give_b, got_a, got_b,
     base_hbm, out_hbm, num_ref, base, out, spread_ref, y_add, x_add, in_sems, out_sems) = refs
    kinds, tile_x, tile_y = base.shape
    levels = kinds // 3
    slots = ys_ref.shape[1]
    blocks = slots // RB
    read = part_copies(base_hbm, base, in_sems, kinds // PARTS)
    each(PARTS, lambda i: read(i).start())
    total = sum_ref[0 : kinds + 1, :] + recv_refs[-1][0 : kinds + 1, :]
    averaged = total[0:kinds] / total[kinds : kinds + 1]
    spread_ref[0:kinds, :] = terms_ref[...] - dot(gram_ref[...], averaged, NN, HIGHEST)
    spread_ref[kinds : kinds + 1, :] = jnp.ones((1, slots), jnp.float32)

    y_blocks = tile_y // YB
    for b in range(y_blocks):
        met = [(bounds_ref[2 * j] <= b) & (b < bounds_ref[2 * j + 1]) for j in range(blocks)]

        @pl.when(jnp.logical_not(functools.reduce(jnp.logical_or, met)))
        def _(b=b):
            num_ref[:, b * YB : (b + 1) * YB, :] = jnp.zeros((kinds + 1, YB, tile_x), jnp.float32)

    before = -1
    for j, b in pair_list(bounds_ref, blocks, y_blocks):
        lanes = pl.ds(pl.multiple_of(j * RB, RB), RB)
        start = pl.multiple_of(jnp.minimum(b, y_blocks - 1) * YB, YB)
        named = (iota((YB, RB), 0) + b * YB).astype(jnp.float32) == ys_ref[0:1, lanes]
        spread = spread_ref[0 : kinds + 1, lanes]
        placed = jnp.where(named[None], spread[:, None, :], 0.0)
        b_hi, b_lo = split2(placed.reshape((kinds + 1) * YB, RB))
        both = dot(b_hi, wt_ref[:, lanes], NT)
        part = both[:, 0:tile_x] + both[:, tile_x:] + dot(b_lo, wt_ref[0:tile_x, lanes], NT)
        fresh = (b != before) & (b < y_blocks)
        before = b
        rows = pl.ds(start, YB)
        num_ref[:, rows, :] = part.reshape(kinds + 1, YB, tile_x) + jnp.where(
            fresh, 0.0, num_ref[:, rows, :]
        )

    wind = 0.5 * time_step * advect_coef
    across = time_step * diffuse_h
    scale = time_step * nudge_gain / jnp.maximum(num_ref[kinds], 1.0)
    v_rows = slice(levels, 2 * levels)
    v_a = jnp.concatenate([give_a[v_rows, :]] * 3, axis=0)
    v_b = jnp.concatenate([give_b[v_rows, :]] * 3, axis=0)
    north = jnp.where(even, got_a[...], got_b[...]) * (across - wind * jnp.where(even, v_a, v_b))
    south = jnp.where(even, got_b[...], got_a[...]) * (across + wind * jnp.where(even, v_b, v_a))
    for k in range(kinds):
        y_add[k, 0:1, :] = south[k : k + 1, :]
        y_add[k, 1:2, :] = north[k : k + 1, :]
        west = jnp.zeros((1, tile_y), jnp.float32)
        east = jnp.zeros((1, tile_y), jnp.float32)
        for s in range(stages):
            partner = me ^ (2 ** (s + 1) - 1)
            west = west + jnp.where(partner == me - 1, recv_refs[s][edge_place(slots, k, 1)], 0.0)
            east = east + jnp.where(partner == me + 1, recv_refs[s][edge_place(slots, k, 0)], 0.0)
        z = k % levels
        x_add[k, 0:1, :] = west * (across + wind * sum_ref[edge_place(slots, z, 0)])
        x_add[k, 1:2, :] = east * (across - wind * sum_ref[edge_place(slots, z, 1)])
    each(PARTS, lambda i: read(i).wait())
    cell_row = iota((tile_y, tile_x), 0)

    def finish(k):
        edges = jnp.where(
            cell_row == 0, y_add[k, 0:1, :], jnp.where(cell_row == tile_y - 1, y_add[k, 1:2, :], 0.0)
        )
        out[k] = base[k] + jnp.transpose(num_ref[k] * scale + edges)
        out[k, 0:1, :] += x_add[k, 0:1, :]
        out[k, tile_x - 1 : tile_x, :] += x_add[k, 1:2, :]
        pltpu.make_async_copy(out.at[k], out_hbm.at[k], out_sems.at[k]).start()

    def finish_some(i):
        for n in range(levels):
            finish(i * levels + n)

    each(kinds // levels, finish_some)
    each(kinds, lambda k: pltpu.make_async_copy(out.at[k], out_hbm.at[k], out_sems.at[k]).wait())


def call(kernel, name, out_shape, in_specs, out_specs, scratch=(), vmem=8, flops=0, moved=0):
    return pl.pallas_call(
        kernel,
        name=name,
        out_shape=out_shape,
        in_specs=in_specs,
        out_specs=out_specs,
        scratch_shapes=list(scratch),
        compiler_params=pltpu.CompilerParams(vmem_limit_bytes=vmem * MIB),
        cost_estimate=pl.CostEstimate(flops=flops, bytes_accessed=moved, transcendentals=0),
    )


def local(model_state, obs_val, obs_owner, obs_x, obs_y, cressman, vertical):
    count_x = lax.axis_size("gx")
    count_y = lax.axis_size("gy")
    fields, levels, tile_x, tile_y = model_state.shape
    kinds = fields * levels
    records = obs_val.shape[0]
    width = cressman.shape[0]
    cap = max(2, 2 * records // count_y)
    slots = count_x * count_y * cap
    blocks = slots // RB
    f32, bf16, i32 = jnp.float32, jnp.bfloat16, jnp.int32
    shape = jax.ShapeDtypeStruct
    stages = count_x.bit_length() - 1

    msg, gram = call(
        functools.partial(pack_kernel, count_y, cap),
        "pack_records",
        (shape((count_x * count_y, 8, LANES), f32), shape((kinds, kinds), f32)),
        [HBM] * 5,
        (VMEM, VMEM),
        [pltpu.VMEM((1, records), i32)] * 3
        + [
            pltpu.VMEM(obs_val.shape, f32),
            pltpu.VMEM((kinds, vertical.shape[2]), f32),
            pltpu.SemaphoreType.DMA((5,)),
        ],
        vmem=MOST,
        flops=10**7,
        moved=10**6,
    )(
        obs_owner.reshape(1, records),
        obs_x.reshape(1, records),
        obs_y.reshape(1, records),
        obs_val,
        vertical.reshape(kinds, vertical.shape[2]),
    )
    recv = lax.all_to_all(msg, ("gx", "gy"), split_axis=0, concat_axis=0, tiled=True)

    base = call(
        stencil_kernel,
        "stencil",
        shape(model_state.shape, f32),
        [HBM],
        HBM,
        [
            pltpu.VMEM(model_state.shape, f32),
            pltpu.VMEM(model_state.shape, f32),
            pltpu.SemaphoreType.DMA((levels,)),
            pltpu.SemaphoreType.DMA((levels,)),
        ],
        vmem=MOST,
        moved=10**7,
    )(model_state)

    state3 = model_state.reshape(kinds, tile_x, tile_y)
    partial, wt, ys, terms, bounds, give_a, give_b = call(
        functools.partial(sums_kernel, cap),
        "column_sums",
        (
            shape((WORDS, slots), f32),
            shape((2 * tile_x, slots), bf16),
            shape((8, slots), f32),
            shape((kinds, slots), f32),
            shape((2 * blocks,), i32),
            shape((kinds, tile_x), f32),
            shape((kinds, tile_x), f32),
        ),
        [VMEM, HBM, HBM, HBM],
        (VMEM, VMEM, VMEM, VMEM, SMEM, VMEM, VMEM),
        [
            pltpu.VMEM((kinds, tile_x, tile_y), f32),
            pltpu.VMEM((width, tile_x), f32),
            pltpu.VMEM((kinds, tile_y, tile_x), bf16),
            pltpu.VMEM((kinds, tile_y, tile_x), bf16),
            pltpu.VMEM((2 * tile_x, width), bf16),
            pltpu.SemaphoreType.DMA((PARTS,)),
            pltpu.SemaphoreType.DMA((PARTS,)),
        ],
        vmem=SOME,
        flops=4 * 10**9,
        moved=10**7,
    )(recv, base, state3, cressman)

    got_a = lax.ppermute(give_a, "gy", [(i, i ^ 1) for i in range(count_y)])
    got_b = lax.ppermute(give_b, "gy", [(i, ((i - 1) ^ 1) + 1) for i in range(1, count_y - 1)])

    summed, received = partial, []
    summing = (jnp.arange(WORDS) < kinds + 1)[:, None]
    for s in range(stages):
        mask = 2 ** (s + 1) - 1
        got = lax.ppermute(summed, "gx", [(i, i ^ mask) for i in range(count_x)])
        received.append(got)
        if s < stages - 1:
            summed = jnp.where(summing, summed + got, summed)

    out = call(
        functools.partial(nudge_kernel, stages),
        "nudge",
        shape((kinds, tile_x, tile_y), f32),
        [SMEM] + [VMEM] * (9 + stages) + [HBM],
        ANY,
        [
            pltpu.VMEM((kinds + 1, tile_y, tile_x), f32),
            pltpu.VMEM((kinds, tile_x, tile_y), f32),
            pltpu.VMEM((kinds, tile_x, tile_y), f32),
            pltpu.VMEM((WORDS, slots), f32),
            pltpu.VMEM((kinds, 2, tile_x), f32),
            pltpu.VMEM((kinds, 2, tile_y), f32),
            pltpu.SemaphoreType.DMA((PARTS,)),
            pltpu.SemaphoreType.DMA((kinds,)),
        ],
        vmem=SOME,
        flops=4 * 10**9,
        moved=10**7,
    )(
        bounds, summed, *received, terms, gram, ys, wt,
        give_a, give_b, got_a, got_b, base.reshape(kinds, tile_x, tile_y),
    )
    return out.reshape(model_state.shape)


def solution(mesh):
    in_specs = (
        P(None, None, "gx", "gy"),
        P(("gx", "gy"), None),
        P(("gx", "gy"), None),
        P(("gx", "gy")),
        P(("gx", "gy")),
        P(None, "gx"),
        P(),
    )
    out_specs = P(None, None, "gx", "gy")
    return jax.shard_map(local, mesh=mesh, in_specs=in_specs, out_specs=out_specs, check_vma=False)
```

```python
import functools

import jax
import jax.numpy as jnp
from jax import lax
from jax.experimental import pallas as pl
from jax.experimental.pallas import tpu as pltpu
from jax.sharding import PartitionSpec as P

advect_coef = 0.5
diffuse_h = 0.2
diffuse_z = 0.1
time_step = 0.5
nudge_gain = 1.0
spread_gain = 0.125

LANES = 128
WORDS = 32
LANE_STEP = 32
YB = 16
PARTS = 4
RB = 256
MIB = 1024 * 1024
MOST = 58
SOME = 50

HIGHEST = lax.Precision.HIGHEST
NT = (((1,), (1,)), ((), ()))
NN = (((1,), (0,)), ((), ()))
VMEM = pl.BlockSpec(memory_space=pltpu.VMEM)
ANY = pl.BlockSpec(memory_space=pl.ANY)
SMEM = pl.BlockSpec(memory_space=pltpu.SMEM)
HBM = pl.BlockSpec(memory_space=pltpu.HBM)


def dot(a, b, dims=NN, precision=None):
    return lax.dot_general(a, b, dims, precision=precision, preferred_element_type=jnp.float32)


def split2(value):
    high = value.astype(jnp.bfloat16)
    low = (value - high.astype(jnp.float32)).astype(jnp.bfloat16)
    return high, low


def dot3(a, b, dims=NN):
    (a_hi, a_lo), (b_hi, b_lo) = [[half.astype(jnp.float32) for half in split2(m)] for m in (a, b)]
    a3 = jnp.concatenate([a_hi, a_hi, a_lo], axis=dims[0][0][0]).astype(jnp.bfloat16)
    b3 = jnp.concatenate([b_hi, b_lo, b_hi], axis=dims[0][1][0]).astype(jnp.bfloat16)
    return dot(a3, b3, dims)


def iota(shape, axis):
    return lax.broadcasted_iota(jnp.int32, shape, axis)


def each(count, action):
    lax.fori_loop(0, count, lambda i, carry: (action(i), carry)[1], 0)


def part_copies(source, target, sem, size):
    def copy(i):
        some = pl.ds(pl.multiple_of(i * size, size), size)
        return pltpu.make_async_copy(source.at[some], target.at[some], sem.at[i])

    return copy


def pack_kernel(count_y, cap, *refs):
    sources, (msg_ref, gram_ref), places, sems = refs[:5], refs[5:7], refs[7:12], refs[12]
    copies = [pltpu.make_async_copy(a, b, sems.at[i]) for i, (a, b) in enumerate(zip(sources, places))]
    for copy in copies:
        copy.start()
    for copy in copies:
        copy.wait()
    owner_ref, x_ref, y_ref, obs_ref, vert_ref = places
    records, kinds = x_ref.shape[1], vert_ref.shape[0]
    levels = kinds // 3
    vert = vert_ref[...]
    terms = []
    for v in range(3):
        obs = obs_ref[:, v * LANES : (v + 1) * LANES]
        terms.append(dot3(vert[v * levels : (v + 1) * levels], obs, NT) * spread_gain)
    row = iota((8, records), 0)
    x_row = jnp.broadcast_to(x_ref[...].astype(jnp.float32), (8, records))
    y_row = jnp.broadcast_to(y_ref[...].astype(jnp.float32) - float(LANES), (8, records))
    head = jnp.where(row % 4 == 0, x_row, jnp.where(row % 4 == 1, y_row, 0.0))
    payload = jnp.concatenate([head] + terms, axis=0)

    owner = owner_ref[...].astype(jnp.float32)
    owner_lanes = jnp.broadcast_to(owner, (records, records))
    owner_rows = jnp.transpose(owner_lanes)
    earlier = iota((records, records), 0) < iota((records, records), 1)
    same = jnp.where((owner_lanes == owner_rows) & earlier, 1.0, 0.0)
    rank = jnp.sum(same, axis=0, keepdims=True)
    slot = owner * float(cap) + rank
    places = count_y * cap
    pick = jnp.where(iota((places, records), 0).astype(jnp.float32) == slot, 1.0, 0.0)
    high = payload.astype(jnp.bfloat16).astype(jnp.float32)
    middle = (payload - high).astype(jnp.bfloat16).astype(jnp.float32)
    parts = jnp.concatenate([high, middle, payload - high - middle], axis=0).astype(jnp.bfloat16)
    out = dot(parts, pick.astype(jnp.bfloat16), NT)
    out = out[0:WORDS] + out[WORDS : 2 * WORDS] + out[2 * WORDS :]

    lane = iota((8, LANES), 1)
    for c in range(count_y):
        chunk = (c * cap) // LANES
        offset = (c * cap) % LANES
        block = jnp.zeros((8, LANES), jnp.float32)
        for j in range(WORDS // 8):
            part = out[8 * j : 8 * j + 8, chunk * LANES : (chunk + 1) * LANES]
            shift = (LANE_STEP * j - offset) % LANES
            if shift:
                part = pltpu.roll(part, shift, 1)
            inside = (lane >= LANE_STEP * j) & (lane < LANE_STEP * j + cap)
            block = jnp.where(inside, part, block)
        for g in range(msg_ref.shape[0] // count_y):
            msg_ref[g * count_y + c] = block[0:4] if g % 2 == 0 else block[4:8]

    gram = dot(vert, vert, NT, HIGHEST) * spread_gain
    alike = (iota((kinds, kinds), 0) // levels) == (iota((kinds, kinds), 1) // levels)
    gram_ref[...] = jnp.where(alike, gram, 0.0)


def unpack(recv_ref, cap, j):
    devices = recv_ref.shape[0]
    per = LANES // cap
    lane = iota((8, LANES), 1)
    chunks = []
    for q in range(devices // per):
        block = jnp.zeros((8, LANES), jnp.float32)
        for t in range(per):
            part = recv_ref[q * per + t]
            shift = (cap * t - LANE_STEP * j) % LANES
            if shift:
                part = pltpu.roll(part, shift, 1)
            inside = (lane >= cap * t) & (lane < cap * t + cap)
            block = jnp.where(inside, part, block)
        chunks.append(block)
    return chunks


def pair_list(bounds_ref, blocks, y_blocks):
    j, b = jnp.int32(0), bounds_ref[0]
    pairs = []
    for _ in range(blocks + y_blocks - 1):
        valid = (j < blocks) & (b < bounds_ref[2 * jnp.minimum(j, blocks - 1) + 1])
        pairs.append((jnp.minimum(j, blocks - 1), jnp.where(valid, b, y_blocks + 1)))
        more = b + 1 < bounds_ref[2 * jnp.minimum(j, blocks - 1) + 1]
        following = jnp.minimum(j + 1, blocks - 1)
        b = jnp.where(more, b + 1, bounds_ref[2 * following])
        j = jnp.where(more, j, jnp.minimum(j + 1, blocks))
    return pairs


def edge_place(slots, k, side):
    per = slots // LANES
    rows = -(-24 // per)
    return pl.ds(25 + side * rows + k // per, 1), pl.ds((k % per) * LANES, LANES)


def sums_kernel(
    cap, recv_ref, base_hbm, state_hbm, cress_hbm,
    msg_ref, wt_ref, ys_ref, terms_ref, bounds_ref, give_a_ref, give_b_ref,
    state, cress, mt_hi, mt_lo, ct, cress_sems, state_sems,
):
    kinds, tile_x, tile_y = state.shape
    width = cress.shape[0]
    cress_read = part_copies(cress_hbm, cress, cress_sems, width // PARTS)
    state_read = part_copies(state_hbm, state, state_sems, kinds // PARTS)
    each(PARTS, lambda i: cress_read(i).start())
    each(PARTS, lambda i: state_read(i).start())
    slots = 2 * recv_ref.shape[0] * cap
    blocks = slots // RB
    chunks = slots // LANES

    groups = [unpack(recv_ref, cap, j) for j in range(WORDS // 8)]
    keys = []
    for c in range(chunks):
        place = (iota((1, LANES), 1) + c * LANES).astype(jnp.float32)
        at = 1 if c < chunks // 2 else 5
        y_row = groups[0][c % (chunks // 2)][at : at + 1]
        keys.append((y_row + float(tile_y)) * float(slots) + place)
    counts = [jnp.zeros((8, LANES), jnp.float32) for _ in range(chunks)]
    for c in range(chunks):
        column = jnp.transpose(jnp.broadcast_to(keys[c], (LANES, LANES)))
        for d in range(chunks):
            less = jnp.where(column < keys[d], 1.0, 0.0)
            counts[d] = counts[d] + jnp.sum(less.reshape(LANES // 8, 8, LANES), axis=0)
    rank = jnp.concatenate([jnp.sum(count, axis=0, keepdims=True) for count in counts], axis=1)

    rows = []
    pairs = [jnp.concatenate(group, axis=1) for group in groups]
    head = jnp.concatenate([pairs[0], pltpu.roll(pairs[0], 4, 0)], axis=1)
    x_high = jnp.floor(head[0:1] * 0.0625)
    row = iota((8, slots), 0)
    top = jnp.where(
        row == 0,
        jnp.broadcast_to(x_high, (8, slots)),
        jnp.where(
            row == 1,
            jnp.broadcast_to(head[0:1] - 16.0 * x_high, (8, slots)),
            jnp.where(row == 2, jnp.broadcast_to(head[1:2] + float(tile_y), (8, slots)), 0.0),
        ),
    )
    lower = iota((8, slots // 2), 0) < 4
    words = jnp.concatenate(
        [
            jnp.concatenate([jnp.where(lower, pair, 0.0), jnp.where(lower, 0.0, pair)], axis=1)
            for pair in pairs[1:]
        ],
        axis=0,
    )
    high = words.astype(jnp.bfloat16).astype(jnp.float32)
    middle = (words - high).astype(jnp.bfloat16).astype(jnp.float32)
    low = words - high - middle
    table = jnp.concatenate([top, high, middle, low], axis=0).astype(jnp.bfloat16)

    even = lax.rem(lax.axis_index("gy"), 2) == 0
    x_rows = []
    for j in range(blocks):
        lanes = slice(j * RB, (j + 1) * RB)
        place = (iota((RB, slots), 0) + j * RB).astype(jnp.float32)
        pick = jnp.where(place == rank, 1.0, 0.0).astype(jnp.bfloat16)
        ordered = dot(table, pick, NT)
        x_rows.append(ordered[0:1] * 16.0 + ordered[1:2])
        ys = ordered[2:3]
        ys_ref[:, lanes] = jnp.broadcast_to(ys, (8, RB))
        terms = ordered[8:32] + ordered[32:56] + ordered[56:80]
        for v in range(3):
            some = terms[8 * v : 8 * v + 8]
            terms_ref[8 * v : 8 * v + 8, lanes] = some + pltpu.roll(some, 4, 0)
        msg_ref[WORDS:, lanes] = terms_ref[:, lanes]
        least = jnp.min(ys).astype(jnp.int32)
        most = jnp.minimum(jnp.max(ys).astype(jnp.int32), tile_y - 1)
        bounds_ref[2 * j] = least // YB
        bounds_ref[2 * j + 1] = most // YB + 1

    each(PARTS, lambda i: cress_read(i).wait())
    for i in range(width // LANES):
        rows = slice(i * LANES, (i + 1) * LANES)
        high, low = split2(jnp.transpose(cress[rows, :]))
        ct[0:tile_x, rows] = high
        ct[tile_x:, rows] = low

    def gather(j):
        hot = jnp.where(iota((width, RB), 0).astype(jnp.float32) == x_rows[j], 1.0, 0.0)
        wt = dot(ct[...], hot.astype(jnp.bfloat16))
        wt_ref[:, j * RB : (j + 1) * RB] = wt.astype(jnp.bfloat16)

    half = blocks // 2
    for j in range(half):
        gather(j)
    each(PARTS, lambda i: state_read(i).wait())
    planes = kinds // (blocks - half)
    for j in range(half, blocks):
        gather(j)
        for k in range((j - half) * planes, (j - half + 1) * planes):
            turned = jnp.transpose(state[k])
            high, low = split2(turned)
            mt_hi[k] = high
            mt_lo[k] = low
            first, last = turned[0:1], turned[tile_y - 1 :]
            give_a_ref[k : k + 1, :] = jnp.where(even, last, first)
            give_b_ref[k : k + 1, :] = jnp.where(even, first, last)

    before = running = None
    y_blocks = tile_y // YB
    for j, b in pair_list(bounds_ref, blocks, y_blocks):
        lanes = pl.ds(pl.multiple_of(j * RB, RB), RB)
        start = pl.multiple_of(jnp.minimum(b, y_blocks - 1) * YB, YB)
        a_hi = mt_hi[:, pl.ds(start, YB), :].reshape(kinds * YB, tile_x)
        a_lo = mt_lo[:, pl.ds(start, YB), :].reshape(kinds * YB, tile_x)
        w_hi = wt_ref[0:tile_x, lanes]
        part = dot(jnp.concatenate([a_hi, a_hi], axis=1), wt_ref[:, lanes]) + dot(a_lo, w_hi)
        named = (iota((YB, RB), 0) + b * YB).astype(jnp.float32) == ys_ref[0:1, lanes]
        kept = jnp.where(named[None], part.reshape(kinds, YB, RB), 0.0)
        summed = jnp.sum(kept[:, :8] + kept[:, 8:], axis=1)
        running = summed if before is None else summed + jnp.where(j == before, running, 0.0)
        before = j
        msg_ref[0:kinds, lanes] = running

    ones = jnp.ones((8, 2 * tile_x), jnp.bfloat16)
    for j in range(blocks):
        lanes = slice(j * RB, (j + 1) * RB)
        total = dot(ones, wt_ref[:, lanes])
        msg_ref[kinds : kinds + 1, lanes] = total[0:1]
    msg_ref[kinds + 1 : WORDS, :] = jnp.zeros((WORDS - kinds - 1, slots), jnp.float32)
    for side, edge in enumerate((0, tile_x - 1)):
        for k in range(kinds):
            msg_ref[edge_place(slots, k, side)] = state[k, edge : edge + 1, :]


def stencil_kernel(state_hbm, out_hbm, state, out, in_sems, out_sems):
    fields, levels, tile_x, tile_y = state.shape

    def read(z):
        return pltpu.make_async_copy(state_hbm.at[:, z], state.at[:, z], in_sems.at[z])

    def write(z):
        return pltpu.make_async_copy(out.at[:, z], out_hbm.at[:, z], out_sems.at[z])

    each(levels, lambda z: read(z).start())
    read(0).wait()
    row = iota((tile_x, tile_y), 0)
    lane = iota((tile_x, tile_y), 1)
    wind = 0.5 * time_step * advect_coef
    across = time_step * diffuse_h
    upward = time_step * diffuse_z
    keep = 1.0 - 4.0 * across - 2.0 * upward

    def level(z):
        @pl.when(z + 1 < levels)
        def _():
            read(z + 1).wait()

        u = wind * state[0, z]
        v = wind * state[1, z]
        east_gain = jnp.where(row == tile_x - 1, 0.0, across - u)
        west_gain = jnp.where(row == 0, 0.0, across + u)
        north_gain = jnp.where(lane == tile_y - 1, 0.0, across - v)
        south_gain = jnp.where(lane == 0, 0.0, across + v)
        for f in range(fields):
            cell = state[f, z]
            stacked = state[f, jnp.minimum(z + 1, levels - 1)] + state[f, jnp.maximum(z - 1, 0)]
            total = keep * cell + upward * stacked
            total = total + east_gain * pltpu.roll(cell, tile_x - 1, 0)
            total = total + west_gain * pltpu.roll(cell, 1, 0)
            total = total + north_gain * pltpu.roll(cell, tile_y - 1, 1)
            total = total + south_gain * pltpu.roll(cell, 1, 1)
            out[f, z] = total
        write(z).start()

    each(levels, level)
    each(levels, lambda z: write(z).wait())


def nudge_kernel(stages, bounds_ref, *refs):
    me = lax.axis_index("gx")
    even = lax.rem(lax.axis_index("gy"), 2) == 0
    sum_ref, recv_refs, refs = refs[0], refs[1 : 1 + stages], refs[1 + stages :]
    (terms_ref, gram_ref, ys_ref, wt_ref, give_a, give_b, got_a, got_b,
     base_hbm, out_hbm, num_ref, base, out, spread_ref, y_add, x_add, in_sems, out_sems) = refs
    kinds, tile_x, tile_y = base.shape
    levels = kinds // 3
    slots = ys_ref.shape[1]
    blocks = slots // RB
    read = part_copies(base_hbm, base, in_sems, kinds // PARTS)
    each(PARTS, lambda i: read(i).start())
    total = sum_ref[0 : kinds + 1, :] + recv_refs[-1][0 : kinds + 1, :]
    averaged = total[0:kinds] / total[kinds : kinds + 1]
    upper = (iota(terms_ref.shape, 0) // (levels // 2)) % 2
    terms = jnp.where(upper == lax.rem(me, 2), terms_ref[...], recv_refs[0][WORDS:, :])
    spread_ref[0:kinds, :] = terms - dot(gram_ref[...], averaged, NN, HIGHEST)
    spread_ref[kinds : kinds + 1, :] = jnp.ones((1, slots), jnp.float32)

    y_blocks = tile_y // YB
    for b in range(y_blocks):
        met = [(bounds_ref[2 * j] <= b) & (b < bounds_ref[2 * j + 1]) for j in range(blocks)]

        @pl.when(jnp.logical_not(functools.reduce(jnp.logical_or, met)))
        def _(b=b):
            num_ref[:, b * YB : (b + 1) * YB, :] = jnp.zeros((kinds + 1, YB, tile_x), jnp.float32)

    before = -1
    for j, b in pair_list(bounds_ref, blocks, y_blocks):
        lanes = pl.ds(pl.multiple_of(j * RB, RB), RB)
        start = pl.multiple_of(jnp.minimum(b, y_blocks - 1) * YB, YB)
        named = (iota((YB, RB), 0) + b * YB).astype(jnp.float32) == ys_ref[0:1, lanes]
        spread = spread_ref[0 : kinds + 1, lanes]
        placed = jnp.where(named[None], spread[:, None, :], 0.0)
        b_hi, b_lo = split2(placed.reshape((kinds + 1) * YB, RB))
        both = dot(b_hi, wt_ref[:, lanes], NT)
        part = both[:, 0:tile_x] + both[:, tile_x:] + dot(b_lo, wt_ref[0:tile_x, lanes], NT)
        fresh = (b != before) & (b < y_blocks)
        before = b
        rows = pl.ds(start, YB)
        num_ref[:, rows, :] = part.reshape(kinds + 1, YB, tile_x) + jnp.where(
            fresh, 0.0, num_ref[:, rows, :]
        )

    wind = 0.5 * time_step * advect_coef
    across = time_step * diffuse_h
    scale = time_step * nudge_gain / jnp.maximum(num_ref[kinds], 1.0)
    v_rows = slice(levels, 2 * levels)
    v_a = jnp.concatenate([give_a[v_rows, :]] * 3, axis=0)
    v_b = jnp.concatenate([give_b[v_rows, :]] * 3, axis=0)
    north = jnp.where(even, got_a[...], got_b[...]) * (across - wind * jnp.where(even, v_a, v_b))
    south = jnp.where(even, got_b[...], got_a[...]) * (across + wind * jnp.where(even, v_b, v_a))
    for k in range(kinds):
        y_add[k, 0:1, :] = south[k : k + 1, :]
        y_add[k, 1:2, :] = north[k : k + 1, :]
        west = jnp.zeros((1, tile_y), jnp.float32)
        east = jnp.zeros((1, tile_y), jnp.float32)
        for s in range(stages):
            partner = me ^ (2 ** (s + 1) - 1)
            west = west + jnp.where(partner == me - 1, recv_refs[s][edge_place(slots, k, 1)], 0.0)
            east = east + jnp.where(partner == me + 1, recv_refs[s][edge_place(slots, k, 0)], 0.0)
        z = k % levels
        x_add[k, 0:1, :] = west * (across + wind * sum_ref[edge_place(slots, z, 0)])
        x_add[k, 1:2, :] = east * (across - wind * sum_ref[edge_place(slots, z, 1)])
    each(PARTS, lambda i: read(i).wait())
    cell_row = iota((tile_y, tile_x), 0)

    def finish(k):
        edges = jnp.where(
            cell_row == 0, y_add[k, 0:1, :], jnp.where(cell_row == tile_y - 1, y_add[k, 1:2, :], 0.0)
        )
        out[k] = base[k] + jnp.transpose(num_ref[k] * scale + edges)
        out[k, 0:1, :] += x_add[k, 0:1, :]
        out[k, tile_x - 1 : tile_x, :] += x_add[k, 1:2, :]
        pltpu.make_async_copy(out.at[k], out_hbm.at[k], out_sems.at[k]).start()

    def finish_some(i):
        for n in range(levels):
            finish(i * levels + n)

    each(kinds // levels, finish_some)
    each(kinds, lambda k: pltpu.make_async_copy(out.at[k], out_hbm.at[k], out_sems.at[k]).wait())


def call(kernel, name, out_shape, in_specs, out_specs, scratch=(), vmem=8, flops=0, moved=0):
    return pl.pallas_call(
        kernel,
        name=name,
        out_shape=out_shape,
        in_specs=in_specs,
        out_specs=out_specs,
        scratch_shapes=list(scratch),
        compiler_params=pltpu.CompilerParams(vmem_limit_bytes=vmem * MIB),
        cost_estimate=pl.CostEstimate(flops=flops, bytes_accessed=moved, transcendentals=0),
    )


def local(model_state, obs_val, obs_owner, obs_x, obs_y, cressman, vertical):
    count_x = lax.axis_size("gx")
    count_y = lax.axis_size("gy")
    fields, levels, tile_x, tile_y = model_state.shape
    kinds = fields * levels
    records = obs_val.shape[0]
    width = cressman.shape[0]
    cap = max(2, 2 * records // count_y)
    slots = count_x * count_y * cap
    blocks = slots // RB
    f32, bf16, i32 = jnp.float32, jnp.bfloat16, jnp.int32
    shape = jax.ShapeDtypeStruct
    stages = count_x.bit_length() - 1

    msg, gram = call(
        functools.partial(pack_kernel, count_y, cap),
        "pack_records",
        (shape((count_x * count_y, 4, LANES), f32), shape((kinds, kinds), f32)),
        [HBM] * 5,
        (VMEM, VMEM),
        [pltpu.VMEM((1, records), i32)] * 3
        + [
            pltpu.VMEM(obs_val.shape, f32),
            pltpu.VMEM((kinds, vertical.shape[2]), f32),
            pltpu.SemaphoreType.DMA((5,)),
        ],
        vmem=MOST,
        flops=10**7,
        moved=10**6,
    )(
        obs_owner.reshape(1, records),
        obs_x.reshape(1, records),
        obs_y.reshape(1, records),
        obs_val,
        vertical.reshape(kinds, vertical.shape[2]),
    )
    recv = lax.all_to_all(msg, ("gx", "gy"), split_axis=0, concat_axis=0, tiled=True)
    recv = recv.reshape(count_x * count_y // 2, 8, LANES)

    base = call(
        stencil_kernel,
        "stencil",
        shape(model_state.shape, f32),
        [HBM],
        HBM,
        [
            pltpu.VMEM(model_state.shape, f32),
            pltpu.VMEM(model_state.shape, f32),
            pltpu.SemaphoreType.DMA((levels,)),
            pltpu.SemaphoreType.DMA((levels,)),
        ],
        vmem=MOST,
        moved=10**7,
    )(model_state)

    state3 = model_state.reshape(kinds, tile_x, tile_y)
    partial, wt, ys, terms, bounds, give_a, give_b = call(
        functools.partial(sums_kernel, cap),
        "column_sums",
        (
            shape((WORDS + kinds, slots), f32),
            shape((2 * tile_x, slots), bf16),
            shape((8, slots), f32),
            shape((kinds, slots), f32),
            shape((2 * blocks,), i32),
            shape((kinds, tile_x), f32),
            shape((kinds, tile_x), f32),
        ),
        [VMEM, HBM, HBM, HBM],
        (VMEM, VMEM, VMEM, VMEM, SMEM, VMEM, VMEM),
        [
            pltpu.VMEM((kinds, tile_x, tile_y), f32),
            pltpu.VMEM((width, tile_x), f32),
            pltpu.VMEM((kinds, tile_y, tile_x), bf16),
            pltpu.VMEM((kinds, tile_y, tile_x), bf16),
            pltpu.VMEM((2 * tile_x, width), bf16),
            pltpu.SemaphoreType.DMA((PARTS,)),
            pltpu.SemaphoreType.DMA((PARTS,)),
        ],
        vmem=SOME,
        flops=4 * 10**9,
        moved=10**7,
    )(recv, base, state3, cressman)

    got_a = lax.ppermute(give_a, "gy", [(i, i ^ 1) for i in range(count_y)])
    got_b = lax.ppermute(give_b, "gy", [(i, ((i - 1) ^ 1) + 1) for i in range(1, count_y - 1)])

    summed, received = partial, []
    summing = (jnp.arange(WORDS) < kinds + 1)[:, None]
    for s in range(stages):
        mask = 2 ** (s + 1) - 1
        got = lax.ppermute(summed, "gx", [(i, i ^ mask) for i in range(count_x)])
        received.append(got)
        if s < stages - 1:
            summed = jnp.where(summing, summed[:WORDS] + got[:WORDS], summed[:WORDS])

    out = call(
        functools.partial(nudge_kernel, stages),
        "nudge",
        shape((kinds, tile_x, tile_y), f32),
        [SMEM] + [VMEM] * (9 + stages) + [HBM],
        ANY,
        [
            pltpu.VMEM((kinds + 1, tile_y, tile_x), f32),
            pltpu.VMEM((kinds, tile_x, tile_y), f32),
            pltpu.VMEM((kinds, tile_x, tile_y), f32),
            pltpu.VMEM((WORDS, slots), f32),
            pltpu.VMEM((kinds, 2, tile_x), f32),
            pltpu.VMEM((kinds, 2, tile_y), f32),
            pltpu.SemaphoreType.DMA((PARTS,)),
            pltpu.SemaphoreType.DMA((kinds,)),
        ],
        vmem=SOME,
        flops=4 * 10**9,
        moved=10**7,
    )(
        bounds, summed, *received, terms, gram, ys, wt,
        give_a, give_b, got_a, got_b, base.reshape(kinds, tile_x, tile_y),
    )
    return out.reshape(model_state.shape)


def solution(mesh):
    in_specs = (
        P(None, None, "gx", "gy"),
        P(("gx", "gy"), None),
        P(("gx", "gy"), None),
        P(("gx", "gy")),
        P(("gx", "gy")),
        P(None, "gx"),
        P(),
    )
    out_specs = P(None, None, "gx", "gy")
    return jax.shard_map(local, mesh=mesh, in_specs=in_specs, out_specs=out_specs, check_vma=False)
```

```python
import functools

import jax
import jax.numpy as jnp
from jax import lax
from jax.experimental import pallas as pl
from jax.experimental.pallas import tpu as pltpu
from jax.sharding import PartitionSpec as P

advect_coef = 0.5
diffuse_h = 0.2
diffuse_z = 0.1
time_step = 0.5
nudge_gain = 1.0
spread_gain = 0.125

LANES = 128
WORDS = 32
LANE_STEP = 32
YB = 16
PARTS = 4
RB = 256
MIB = 1024 * 1024
MOST = 58
SOME = 50

HIGHEST = lax.Precision.HIGHEST
NT = (((1,), (1,)), ((), ()))
NN = (((1,), (0,)), ((), ()))
VMEM = pl.BlockSpec(memory_space=pltpu.VMEM)
ANY = pl.BlockSpec(memory_space=pl.ANY)
SMEM = pl.BlockSpec(memory_space=pltpu.SMEM)
HBM = pl.BlockSpec(memory_space=pltpu.HBM)


def dot(a, b, dims=NN, precision=None):
    return lax.dot_general(a, b, dims, precision=precision, preferred_element_type=jnp.float32)


def split2(value):
    high = value.astype(jnp.bfloat16)
    low = (value - high.astype(jnp.float32)).astype(jnp.bfloat16)
    return high, low


def dot3(a, b, dims=NN):
    (a_hi, a_lo), (b_hi, b_lo) = [[half.astype(jnp.float32) for half in split2(m)] for m in (a, b)]
    a3 = jnp.concatenate([a_hi, a_hi, a_lo], axis=dims[0][0][0]).astype(jnp.bfloat16)
    b3 = jnp.concatenate([b_hi, b_lo, b_hi], axis=dims[0][1][0]).astype(jnp.bfloat16)
    return dot(a3, b3, dims)


def iota(shape, axis):
    return lax.broadcasted_iota(jnp.int32, shape, axis)


def each(count, action):
    lax.fori_loop(0, count, lambda i, carry: (action(i), carry)[1], 0)


def part_copies(source, target, sem, size):
    def copy(i):
        some = pl.ds(pl.multiple_of(i * size, size), size)
        return pltpu.make_async_copy(source.at[some], target.at[some], sem.at[i])

    return copy


def pack_kernel(count_y, cap, *refs):
    sources, (msg_ref, gram_ref), places, sems = refs[:5], refs[5:7], refs[7:12], refs[12]
    copies = [pltpu.make_async_copy(a, b, sems.at[i]) for i, (a, b) in enumerate(zip(sources, places))]
    for copy in copies:
        copy.start()
    for copy in copies:
        copy.wait()
    owner_ref, x_ref, y_ref, obs_ref, vert_ref = places
    records, kinds = x_ref.shape[1], vert_ref.shape[0]
    levels = kinds // 3
    vert = vert_ref[...]
    terms = []
    for v in range(3):
        obs = obs_ref[:, v * LANES : (v + 1) * LANES]
        terms.append(dot3(vert[v * levels : (v + 1) * levels], obs, NT) * spread_gain)
    row = iota((8, records), 0)
    x_row = jnp.broadcast_to(x_ref[...].astype(jnp.float32), (8, records))
    y_row = jnp.broadcast_to(y_ref[...].astype(jnp.float32) - float(LANES), (8, records))
    head = jnp.where(row % 4 == 0, x_row, jnp.where(row % 4 == 1, y_row, 0.0))
    payload = jnp.concatenate([head] + terms, axis=0)

    owner = owner_ref[...].astype(jnp.float32)
    owner_lanes = jnp.broadcast_to(owner, (records, records))
    owner_rows = jnp.transpose(owner_lanes)
    earlier = iota((records, records), 0) < iota((records, records), 1)
    same = jnp.where((owner_lanes == owner_rows) & earlier, 1.0, 0.0)
    rank = jnp.sum(same, axis=0, keepdims=True)
    slot = owner * float(cap) + rank
    places = count_y * cap
    pick = jnp.where(iota((places, records), 0).astype(jnp.float32) == slot, 1.0, 0.0)
    high = payload.astype(jnp.bfloat16).astype(jnp.float32)
    middle = (payload - high).astype(jnp.bfloat16).astype(jnp.float32)
    parts = jnp.concatenate([high, middle, payload - high - middle], axis=0).astype(jnp.bfloat16)
    out = dot(parts, pick.astype(jnp.bfloat16), NT)
    out = out[0:WORDS] + out[WORDS : 2 * WORDS] + out[2 * WORDS :]

    lane = iota((8, LANES), 1)
    for c in range(count_y):
        chunk = (c * cap) // LANES
        offset = (c * cap) % LANES
        block = jnp.zeros((8, LANES), jnp.float32)
        for j in range(WORDS // 8):
            part = out[8 * j : 8 * j + 8, chunk * LANES : (chunk + 1) * LANES]
            shift = (LANE_STEP * j - offset) % LANES
            if shift:
                part = pltpu.roll(part, shift, 1)
            inside = (lane >= LANE_STEP * j) & (lane < LANE_STEP * j + cap)
            block = jnp.where(inside, part, block)
        for g in range(msg_ref.shape[0] // count_y):
            msg_ref[g * count_y + c] = block[0:4] if g % 2 == 0 else block[4:8]

    gram = dot(vert, vert, NT, HIGHEST) * spread_gain
    alike = (iota((kinds, kinds), 0) // levels) == (iota((kinds, kinds), 1) // levels)
    gram_ref[...] = jnp.where(alike, gram, 0.0)


def unpack(recv_ref, cap, j):
    devices = recv_ref.shape[0]
    per = LANES // cap
    lane = iota((8, LANES), 1)
    chunks = []
    for q in range(devices // per):
        block = jnp.zeros((8, LANES), jnp.float32)
        for t in range(per):
            part = recv_ref[q * per + t]
            shift = (cap * t - LANE_STEP * j) % LANES
            if shift:
                part = pltpu.roll(part, shift, 1)
            inside = (lane >= cap * t) & (lane < cap * t + cap)
            block = jnp.where(inside, part, block)
        chunks.append(block)
    return chunks


def pair_list(bounds_ref, blocks, y_blocks):
    j, b = jnp.int32(0), bounds_ref[0]
    pairs = []
    for _ in range(blocks + y_blocks - 1):
        valid = (j < blocks) & (b < bounds_ref[2 * jnp.minimum(j, blocks - 1) + 1])
        pairs.append((jnp.minimum(j, blocks - 1), jnp.where(valid, b, y_blocks + 1)))
        more = b + 1 < bounds_ref[2 * jnp.minimum(j, blocks - 1) + 1]
        following = jnp.minimum(j + 1, blocks - 1)
        b = jnp.where(more, b + 1, bounds_ref[2 * following])
        j = jnp.where(more, j, jnp.minimum(j + 1, blocks))
    return pairs


def edge_place(slots, k, side):
    per = slots // LANES
    rows = -(-24 // per)
    return pl.ds(25 + side * rows + k // per, 1), pl.ds((k % per) * LANES, LANES)


def sums_kernel(
    cap, recv_ref, base_hbm, state_hbm, cress_hbm,
    msg_ref, wt_ref, ys_ref, terms_ref, bounds_ref, give_a_ref, give_b_ref,
    state, cress, mt_hi, mt_lo, ct, cress_sems, state_sems,
):
    kinds, tile_x, tile_y = state.shape
    width = cress.shape[0]
    cress_read = part_copies(cress_hbm, cress, cress_sems, width // PARTS)
    state_read = part_copies(state_hbm, state, state_sems, kinds // PARTS)
    each(PARTS, lambda i: cress_read(i).start())
    each(PARTS, lambda i: state_read(i).start())
    slots = 2 * recv_ref.shape[0] * cap
    blocks = slots // RB
    chunks = slots // LANES

    groups = [unpack(recv_ref, cap, j) for j in range(WORDS // 8)]
    keys = []
    for c in range(chunks):
        place = (iota((1, LANES), 1) + c * LANES).astype(jnp.float32)
        at = 1 if c < chunks // 2 else 5
        y_row = groups[0][c % (chunks // 2)][at : at + 1]
        keys.append((y_row + float(tile_y)) * float(slots) + place)
    counts = [jnp.zeros((8, LANES), jnp.float32) for _ in range(chunks)]
    for c in range(chunks):
        column = jnp.transpose(jnp.broadcast_to(keys[c], (LANES, LANES)))
        for d in range(chunks):
            less = jnp.where(column < keys[d], 1.0, 0.0)
            counts[d] = counts[d] + jnp.sum(less.reshape(LANES // 8, 8, LANES), axis=0)
    rank = jnp.concatenate([jnp.sum(count, axis=0, keepdims=True) for count in counts], axis=1)

    rows = []
    pairs = [jnp.concatenate(group, axis=1) for group in groups]
    head = jnp.concatenate([pairs[0], pltpu.roll(pairs[0], 4, 0)], axis=1)
    x_high = jnp.floor(head[0:1] * 0.0625)
    row = iota((8, slots), 0)
    top = jnp.where(
        row == 0,
        jnp.broadcast_to(x_high, (8, slots)),
        jnp.where(
            row == 1,
            jnp.broadcast_to(head[0:1] - 16.0 * x_high, (8, slots)),
            jnp.where(row == 2, jnp.broadcast_to(head[1:2] + float(tile_y), (8, slots)), 0.0),
        ),
    )
    lower = iota((8, slots // 2), 0) < 4
    words = jnp.concatenate(
        [
            jnp.concatenate([jnp.where(lower, pair, 0.0), jnp.where(lower, 0.0, pair)], axis=1)
            for pair in pairs[1:]
        ],
        axis=0,
    )
    high = words.astype(jnp.bfloat16).astype(jnp.float32)
    middle = (words - high).astype(jnp.bfloat16).astype(jnp.float32)
    low = words - high - middle
    table = jnp.concatenate([top, high, middle, low], axis=0).astype(jnp.bfloat16)

    even = lax.rem(lax.axis_index("gy"), 2) == 0
    x_rows = []
    for j in range(blocks):
        lanes = slice(j * RB, (j + 1) * RB)
        place = (iota((RB, slots), 0) + j * RB).astype(jnp.float32)
        pick = jnp.where(place == rank, 1.0, 0.0).astype(jnp.bfloat16)
        ordered = dot(table, pick, NT)
        x_rows.append(ordered[0:1] * 16.0 + ordered[1:2])
        ys = ordered[2:3]
        ys_ref[:, lanes] = jnp.broadcast_to(ys, (8, RB))
        terms = ordered[8:32] + ordered[32:56] + ordered[56:80]
        for v in range(3):
            some = terms[8 * v : 8 * v + 8]
            terms_ref[8 * v : 8 * v + 8, lanes] = some + pltpu.roll(some, 4, 0)
        msg_ref[WORDS:, lanes] = terms_ref[:, lanes]
        least = jnp.min(ys).astype(jnp.int32)
        most = jnp.minimum(jnp.max(ys).astype(jnp.int32), tile_y - 1)
        bounds_ref[2 * j] = least // YB
        bounds_ref[2 * j + 1] = most // YB + 1

    each(PARTS, lambda i: cress_read(i).wait())
    for i in range(width // LANES):
        rows = slice(i * LANES, (i + 1) * LANES)
        high, low = split2(jnp.transpose(cress[rows, :]))
        ct[0:tile_x, rows] = high
        ct[tile_x:, rows] = low

    def gather(j):
        hot = jnp.where(iota((width, RB), 0).astype(jnp.float32) == x_rows[j], 1.0, 0.0)
        wt = dot(ct[...], hot.astype(jnp.bfloat16))
        wt_ref[:, j * RB : (j + 1) * RB] = wt.astype(jnp.bfloat16)
        msg_ref[kinds : kinds + 1, j * RB : (j + 1) * RB] = jnp.sum(wt, axis=0, keepdims=True)

    half = blocks // 2
    for j in range(half):
        gather(j)
    each(PARTS, lambda i: state_read(i).wait())
    planes = kinds // (blocks - half)
    for j in range(half, blocks):
        gather(j)
        for k in range((j - half) * planes, (j - half + 1) * planes):
            turned = jnp.transpose(state[k])
            high, low = split2(turned)
            mt_hi[k] = high
            mt_lo[k] = low
            first, last = turned[0:1], turned[tile_y - 1 :]
            give_a_ref[k : k + 1, :] = jnp.where(even, last, first)
            give_b_ref[k : k + 1, :] = jnp.where(even, first, last)

    before = running = None
    y_blocks = tile_y // YB
    for j, b in pair_list(bounds_ref, blocks, y_blocks):
        lanes = pl.ds(pl.multiple_of(j * RB, RB), RB)
        start = pl.multiple_of(jnp.minimum(b, y_blocks - 1) * YB, YB)
        a_hi = mt_hi[:, pl.ds(start, YB), :].reshape(kinds * YB, tile_x)
        a_lo = mt_lo[:, pl.ds(start, YB), :].reshape(kinds * YB, tile_x)
        w_hi = wt_ref[0:tile_x, lanes]
        part = dot(jnp.concatenate([a_hi, a_hi], axis=1), wt_ref[:, lanes]) + dot(a_lo, w_hi)
        named = (iota((YB, RB), 0) + b * YB).astype(jnp.float32) == ys_ref[0:1, lanes]
        kept = jnp.where(named[None], part.reshape(kinds, YB, RB), 0.0)
        summed = jnp.sum(kept[:, :8] + kept[:, 8:], axis=1)
        running = summed if before is None else summed + jnp.where(j == before, running, 0.0)
        before = j
        msg_ref[0:kinds, lanes] = running

    msg_ref[kinds + 1 : WORDS, :] = jnp.zeros((WORDS - kinds - 1, slots), jnp.float32)
    for side, edge in enumerate((0, tile_x - 1)):
        for k in range(kinds):
            msg_ref[edge_place(slots, k, side)] = state[k, edge : edge + 1, :]


def stencil_kernel(state_hbm, out_hbm, state, out, in_sems, out_sems):
    fields, levels, tile_x, tile_y = state.shape

    def read(z):
        return pltpu.make_async_copy(state_hbm.at[:, z], state.at[:, z], in_sems.at[z])

    def write(z):
        return pltpu.make_async_copy(out.at[:, z], out_hbm.at[:, z], out_sems.at[z])

    each(levels, lambda z: read(z).start())
    read(0).wait()
    row = iota((tile_x, tile_y), 0)
    lane = iota((tile_x, tile_y), 1)
    wind = 0.5 * time_step * advect_coef
    across = time_step * diffuse_h
    upward = time_step * diffuse_z
    keep = 1.0 - 4.0 * across - 2.0 * upward

    def level(z):
        @pl.when(z + 1 < levels)
        def _():
            read(z + 1).wait()

        u = wind * state[0, z]
        v = wind * state[1, z]
        east_gain = jnp.where(row == tile_x - 1, 0.0, across - u)
        west_gain = jnp.where(row == 0, 0.0, across + u)
        north_gain = jnp.where(lane == tile_y - 1, 0.0, across - v)
        south_gain = jnp.where(lane == 0, 0.0, across + v)
        for f in range(fields):
            cell = state[f, z]
            stacked = state[f, jnp.minimum(z + 1, levels - 1)] + state[f, jnp.maximum(z - 1, 0)]
            total = keep * cell + upward * stacked
            total = total + east_gain * pltpu.roll(cell, tile_x - 1, 0)
            total = total + west_gain * pltpu.roll(cell, 1, 0)
            total = total + north_gain * pltpu.roll(cell, tile_y - 1, 1)
            total = total + south_gain * pltpu.roll(cell, 1, 1)
            out[f, z] = total
        write(z).start()

    each(levels, level)
    each(levels, lambda z: write(z).wait())


def nudge_kernel(stages, bounds_ref, *refs):
    me = lax.axis_index("gx")
    even = lax.rem(lax.axis_index("gy"), 2) == 0
    sum_ref, recv_refs, refs = refs[0], refs[1 : 1 + stages], refs[1 + stages :]
    (terms_ref, gram_ref, ys_ref, wt_ref, give_a, give_b, got_a, got_b,
     base_hbm, out_hbm, num_ref, base, out, spread_ref, y_add, x_add, in_sems, out_sems) = refs
    kinds, tile_x, tile_y = base.shape
    levels = kinds // 3
    slots = ys_ref.shape[1]
    blocks = slots // RB
    read = part_copies(base_hbm, base, in_sems, kinds // PARTS)
    each(PARTS, lambda i: read(i).start())
    total = sum_ref[0 : kinds + 1, :] + recv_refs[-1][0 : kinds + 1, :]
    averaged = total[0:kinds] / total[kinds : kinds + 1]
    upper = (iota(terms_ref.shape, 0) // (levels // 2)) % 2
    terms = jnp.where(upper == lax.rem(me, 2), terms_ref[...], recv_refs[0][WORDS:, :])
    spread_ref[0:kinds, :] = terms - dot(gram_ref[...], averaged, NN, HIGHEST)
    spread_ref[kinds : kinds + 1, :] = jnp.ones((1, slots), jnp.float32)

    y_blocks = tile_y // YB
    for b in range(y_blocks):
        met = [(bounds_ref[2 * j] <= b) & (b < bounds_ref[2 * j + 1]) for j in range(blocks)]

        @pl.when(jnp.logical_not(functools.reduce(jnp.logical_or, met)))
        def _(b=b):
            num_ref[:, b * YB : (b + 1) * YB, :] = jnp.zeros((kinds + 1, YB, tile_x), jnp.float32)

    before = -1
    for j, b in pair_list(bounds_ref, blocks, y_blocks):
        lanes = pl.ds(pl.multiple_of(j * RB, RB), RB)
        start = pl.multiple_of(jnp.minimum(b, y_blocks - 1) * YB, YB)
        named = (iota((YB, RB), 0) + b * YB).astype(jnp.float32) == ys_ref[0:1, lanes]
        spread = spread_ref[0 : kinds + 1, lanes]
        placed = jnp.where(named[None], spread[:, None, :], 0.0)
        b_hi, b_lo = split2(placed.reshape((kinds + 1) * YB, RB))
        both = dot(b_hi, wt_ref[:, lanes], NT)
        part = both[:, 0:tile_x] + both[:, tile_x:] + dot(b_lo, wt_ref[0:tile_x, lanes], NT)
        fresh = (b != before) & (b < y_blocks)
        before = b
        rows = pl.ds(start, YB)
        num_ref[:, rows, :] = part.reshape(kinds + 1, YB, tile_x) + jnp.where(
            fresh, 0.0, num_ref[:, rows, :]
        )

    wind = 0.5 * time_step * advect_coef
    across = time_step * diffuse_h
    scale = time_step * nudge_gain / jnp.maximum(num_ref[kinds], 1.0)
    v_rows = slice(levels, 2 * levels)
    v_a = jnp.concatenate([give_a[v_rows, :]] * 3, axis=0)
    v_b = jnp.concatenate([give_b[v_rows, :]] * 3, axis=0)
    north = jnp.where(even, got_a[...], got_b[...]) * (across - wind * jnp.where(even, v_a, v_b))
    south = jnp.where(even, got_b[...], got_a[...]) * (across + wind * jnp.where(even, v_b, v_a))
    for k in range(kinds):
        y_add[k, 0:1, :] = south[k : k + 1, :]
        y_add[k, 1:2, :] = north[k : k + 1, :]
        west = jnp.zeros((1, tile_y), jnp.float32)
        east = jnp.zeros((1, tile_y), jnp.float32)
        for s in range(stages):
            partner = me ^ (2 ** (s + 1) - 1)
            west = west + jnp.where(partner == me - 1, recv_refs[s][edge_place(slots, k, 1)], 0.0)
            east = east + jnp.where(partner == me + 1, recv_refs[s][edge_place(slots, k, 0)], 0.0)
        z = k % levels
        x_add[k, 0:1, :] = west * (across + wind * sum_ref[edge_place(slots, z, 0)])
        x_add[k, 1:2, :] = east * (across - wind * sum_ref[edge_place(slots, z, 1)])
    each(PARTS, lambda i: read(i).wait())
    cell_row = iota((tile_y, tile_x), 0)

    def finish(k):
        edges = jnp.where(
            cell_row == 0, y_add[k, 0:1, :], jnp.where(cell_row == tile_y - 1, y_add[k, 1:2, :], 0.0)
        )
        out[k] = base[k] + jnp.transpose(num_ref[k] * scale + edges)
        out[k, 0:1, :] += x_add[k, 0:1, :]
        out[k, tile_x - 1 : tile_x, :] += x_add[k, 1:2, :]
        pltpu.make_async_copy(out.at[k], out_hbm.at[k], out_sems.at[k]).start()

    def finish_some(i):
        for n in range(levels):
            finish(i * levels + n)

    each(kinds // levels, finish_some)
    each(kinds, lambda k: pltpu.make_async_copy(out.at[k], out_hbm.at[k], out_sems.at[k]).wait())


def call(kernel, name, out_shape, in_specs, out_specs, scratch=(), vmem=8, flops=0, moved=0):
    return pl.pallas_call(
        kernel,
        name=name,
        out_shape=out_shape,
        in_specs=in_specs,
        out_specs=out_specs,
        scratch_shapes=list(scratch),
        compiler_params=pltpu.CompilerParams(vmem_limit_bytes=vmem * MIB),
        cost_estimate=pl.CostEstimate(flops=flops, bytes_accessed=moved, transcendentals=0),
    )


def local(model_state, obs_val, obs_owner, obs_x, obs_y, cressman, vertical):
    count_x = lax.axis_size("gx")
    count_y = lax.axis_size("gy")
    fields, levels, tile_x, tile_y = model_state.shape
    kinds = fields * levels
    records = obs_val.shape[0]
    width = cressman.shape[0]
    cap = max(2, 2 * records // count_y)
    slots = count_x * count_y * cap
    blocks = slots // RB
    f32, bf16, i32 = jnp.float32, jnp.bfloat16, jnp.int32
    shape = jax.ShapeDtypeStruct
    stages = count_x.bit_length() - 1

    msg, gram = call(
        functools.partial(pack_kernel, count_y, cap),
        "pack_records",
        (shape((count_x * count_y, 4, LANES), f32), shape((kinds, kinds), f32)),
        [HBM] * 5,
        (VMEM, VMEM),
        [pltpu.VMEM((1, records), i32)] * 3
        + [
            pltpu.VMEM(obs_val.shape, f32),
            pltpu.VMEM((kinds, vertical.shape[2]), f32),
            pltpu.SemaphoreType.DMA((5,)),
        ],
        vmem=MOST,
        flops=10**7,
        moved=10**6,
    )(
        obs_owner.reshape(1, records),
        obs_x.reshape(1, records),
        obs_y.reshape(1, records),
        obs_val,
        vertical.reshape(kinds, vertical.shape[2]),
    )
    recv = lax.all_to_all(msg, ("gx", "gy"), split_axis=0, concat_axis=0, tiled=True)
    recv = recv.reshape(count_x * count_y // 2, 8, LANES)

    base = call(
        stencil_kernel,
        "stencil",
        shape(model_state.shape, f32),
        [HBM],
        HBM,
        [
            pltpu.VMEM(model_state.shape, f32),
            pltpu.VMEM(model_state.shape, f32),
            pltpu.SemaphoreType.DMA((levels,)),
            pltpu.SemaphoreType.DMA((levels,)),
        ],
        vmem=MOST,
        moved=10**7,
    )(model_state)

    state3 = model_state.reshape(kinds, tile_x, tile_y)
    partial, wt, ys, terms, bounds, give_a, give_b = call(
        functools.partial(sums_kernel, cap),
        "column_sums",
        (
            shape((WORDS + kinds, slots), f32),
            shape((2 * tile_x, slots), bf16),
            shape((8, slots), f32),
            shape((kinds, slots), f32),
            shape((2 * blocks,), i32),
            shape((kinds, tile_x), f32),
            shape((kinds, tile_x), f32),
        ),
        [VMEM, HBM, HBM, HBM],
        (VMEM, VMEM, VMEM, VMEM, SMEM, VMEM, VMEM),
        [
            pltpu.VMEM((kinds, tile_x, tile_y), f32),
            pltpu.VMEM((width, tile_x), f32),
            pltpu.VMEM((kinds, tile_y, tile_x), bf16),
            pltpu.VMEM((kinds, tile_y, tile_x), bf16),
            pltpu.VMEM((2 * tile_x, width), bf16),
            pltpu.SemaphoreType.DMA((PARTS,)),
            pltpu.SemaphoreType.DMA((PARTS,)),
        ],
        vmem=SOME,
        flops=4 * 10**9,
        moved=10**7,
    )(recv, base, state3, cressman)

    got_a = lax.ppermute(give_a, "gy", [(i, i ^ 1) for i in range(count_y)])
    got_b = lax.ppermute(give_b, "gy", [(i, ((i - 1) ^ 1) + 1) for i in range(1, count_y - 1)])

    summed, received = partial, []
    summing = (jnp.arange(WORDS) < kinds + 1)[:, None]
    for s in range(stages):
        mask = 2 ** (s + 1) - 1
        got = lax.ppermute(summed, "gx", [(i, i ^ mask) for i in range(count_x)])
        received.append(got)
        if s < stages - 1:
            summed = jnp.where(summing, summed[:WORDS] + got[:WORDS], summed[:WORDS])

    out = call(
        functools.partial(nudge_kernel, stages),
        "nudge",
        shape((kinds, tile_x, tile_y), f32),
        [SMEM] + [VMEM] * (9 + stages) + [HBM],
        ANY,
        [
            pltpu.VMEM((kinds + 1, tile_y, tile_x), f32),
            pltpu.VMEM((kinds, tile_x, tile_y), f32),
            pltpu.VMEM((kinds, tile_x, tile_y), f32),
            pltpu.VMEM((WORDS, slots), f32),
            pltpu.VMEM((kinds, 2, tile_x), f32),
            pltpu.VMEM((kinds, 2, tile_y), f32),
            pltpu.SemaphoreType.DMA((PARTS,)),
            pltpu.SemaphoreType.DMA((kinds,)),
        ],
        vmem=SOME,
        flops=4 * 10**9,
        moved=10**7,
    )(
        bounds, summed, *received, terms, gram, ys, wt,
        give_a, give_b, got_a, got_b, base.reshape(kinds, tile_x, tile_y),
    )
    return out.reshape(model_state.shape)


def solution(mesh):
    in_specs = (
        P(None, None, "gx", "gy"),
        P(("gx", "gy"), None),
        P(("gx", "gy"), None),
        P(("gx", "gy")),
        P(("gx", "gy")),
        P(None, "gx"),
        P(),
    )
    out_specs = P(None, None, "gx", "gy")
    return jax.shard_map(local, mesh=mesh, in_specs=in_specs, out_specs=out_specs, check_vma=False)
```
